32 devices in a mesh: groups: 2 (over x), tensor: 16 (over z, y, core).
Axes of the slice: x: 2, y: 2, z: 4, core: 2. Of those that a mesh axis runs over, the one named last changes fastest.
Arguments:
- tokens: bfloat16 [64, 8192], P(('groups', 'tensor')), parts along dimension 0, may hold values from -6 to 6
- gate_weight: bfloat16 [8192, 28672], P(None, 'tensor'), may hold values from -0.0625 to 0.0625
- up_weight: bfloat16 [8192, 28672], P(None, 'tensor'), may hold values from -0.0625 to 0.0625
- down_weight: bfloat16 [28672, 8192], P('tensor'), may hold values from -0.03125 to 0.03125
Outputs:
- mixed: bfloat16 [64, 8192], P(('groups', 'tensor')), parts along dimension 0
The draws below stay inside these ranges and needn't reach their ends.
There are 2 independent parts, one for each index of `groups`. The reference program is written for one: setup_inputs(seed, part) draws one part's arguments, and reference() takes and returns one part's arrays. A program takes and returns all parts, laid end to end along the dimension named above; an argument that names none is the same for every part. Nothing has to cross between parts.
All inputs are finite; a program needn't handle non-finite values.
Results may differ from the reference program's by a relative error of at most 0.015.
Values may be sent and summed in bfloat16 or wider, within the bound.
No kernel may reach another device: no remote copies, remote signals or barrier semaphores. Data moves between devices by JAX's collectives and lax.ppermute only.
A program may use at most 128 MiB of HBM per device.

```python
import jax
import jax.numpy as jnp
import numpy as np
from jax import lax

D = 8192
FF = 28672
BLOCK = 32
TOKENS = 32
N_TENSOR = 16


def level_of(own_key, shape, pieces, low, top_value):
    def one(position, shards_of):
        heights = jax.random.uniform(jax.random.fold_in(jax.random.fold_in(own_key, 6), position), (shards_of,), jnp.float32, low / len(pieces), top_value / len(pieces))
        return jnp.repeat(jnp.exp(heights), shape[position] // shards_of).reshape((-1,) + (1,) * (len(shape) - position - 1))

    factor_of = one(*pieces[0])
    for cut in pieces[1:]:
        factor_of = factor_of * one(*cut)
    return factor_of


def normal_values(key, dims, spread, reach, pieces=(), kind=jnp.bfloat16):
    result = spread * jax.random.normal(key, dims, jnp.float32)
    if pieces:
        result = result * level_of(key, dims, pieces, -0.22, 0.18)
    return jnp.clip(result, -reach, reach).astype(kind)


def setup_inputs(seed: int = 0, part: int = 0) -> dict:
    keys = jax.random.split(jax.random.key(seed), 5)
    part_keys = jax.random.split(jax.random.fold_in(keys[4], part), 5)
    return {
        "tokens": normal_values(part_keys[0], (TOKENS, D), 1.0, 6.0, ((0, 16),)),
        "gate_weight": normal_values(keys[1], (D, FF), D ** -0.5, 0.0625, ((1, 16),)),
        "up_weight": normal_values(keys[2], (D, FF), D ** -0.5, 0.0625, ((1, 16),)),
        "down_weight": normal_values(keys[3], (FF, D), FF ** -0.5, 0.03125, ((0, 16),)),
    }


def walsh(order):
    index = np.arange(order)
    common = index[:, None] & index[None, :]
    parity = common * 0
    for shift in range(max(order.bit_length(), 1)):
        parity = parity ^ common >> shift & 1
    return (1 - 2 * parity).astype(np.float32)

def reference(tokens, gate_weight, up_weight, down_weight):
    gate = jnp.dot(tokens, gate_weight, preferred_element_type=jnp.float32)
    up = jnp.dot(tokens, up_weight, preferred_element_type=jnp.float32)
    hidden = jax.nn.silu(gate) * up
    width = FF // N_TENSOR
    shaped = hidden.reshape(TOKENS, N_TENSOR, width // BLOCK, BLOCK)
    outer = jnp.asarray(walsh(N_TENSOR), jnp.float32)
    inner = jnp.asarray(walsh(BLOCK), jnp.float32)
    turned = jnp.einsum('pq,tqbr,rs->tpbs', outer, shaped, inner, precision=lax.Precision.HIGHEST)
    turned = turned * (1.0 / np.sqrt(N_TENSOR * BLOCK))
    rotated = turned.reshape(TOKENS, FF).astype(jnp.bfloat16)
    return jnp.dot(rotated, down_weight, preferred_element_type=jnp.float32).astype(jnp.bfloat16)
```

```python
import jax
import jax.numpy as jnp
import numpy as np
from jax import lax
from jax.sharding import PartitionSpec as P

BLOCK = 32


def swapped(value, axis, stride):
    mask = 2**stride
    pairs = [(source, source ^ mask) for source in range(lax.axis_size(axis))]
    return lax.ppermute(value, axis, pairs)


def walsh(order):
    index = np.arange(order)
    common = index[:, None] & index[None, :]
    parity = common * 0
    for shift in range(max(order.bit_length(), 1)):
        parity = parity ^ common >> shift & 1
    return (1 - 2 * parity).astype(np.float32)


def per_device(tokens, gate_weight, up_weight, down_weight):
    devices = lax.axis_size("tensor")
    levels = devices.bit_length() - 1
    width = gate_weight.shape[1]
    own = tokens.shape[0]
    scale = 1.0 / np.sqrt(devices * BLOCK)
    inner = jnp.asarray(walsh(BLOCK), jnp.float32)
    index = lax.axis_index("tensor")
    upper = [(index >> level) & 1 for level in range(levels)]

    order = list(range(levels))[::-1]
    piece = tokens
    for level in order:
        other = swapped(piece, "tensor", level)
        low = jnp.where(upper[level] == 1, other, piece)
        high = jnp.where(upper[level] == 1, piece, other)
        piece = jnp.concatenate([low, high], axis=0)

    gate = jnp.dot(piece, gate_weight, preferred_element_type=jnp.float32)
    up = jnp.dot(piece, up_weight, preferred_element_type=jnp.float32)
    hidden = jax.nn.silu(gate) * up
    total = hidden.shape[0]
    local = jnp.einsum(
        "tbr,rs->tbs",
        hidden.reshape(total, width // BLOCK, BLOCK),
        inner,
        precision=lax.Precision.HIGHEST,
    ).reshape(total, width)
    for level in range(levels):
        partner = swapped(local.astype(jnp.bfloat16), "tensor", level).astype(local.dtype)
        local = jnp.where(upper[level] == 1, partner - local, local + partner)
    rotated = (local * scale).astype(jnp.bfloat16)
    terms = jnp.dot(rotated, down_weight, preferred_element_type=jnp.float32)

    for level in order[::-1]:
        half = terms.shape[0] // 2
        low, high = terms[:half], terms[half:]
        keep = jnp.where(upper[level] == 1, high, low)
        send = jnp.where(upper[level] == 1, low, high)
        got = swapped(send.astype(jnp.bfloat16), "tensor", level)
        terms = keep + got.astype(jnp.float32)
    return terms.astype(jnp.bfloat16)


def solution(mesh):
    return jax.shard_map(
        per_device,
        mesh=mesh,
        in_specs=(
            P(("groups", "tensor"), None),
            P(None, "tensor"),
            P(None, "tensor"),
            P("tensor", None),
        ),
        out_specs=P(("groups", "tensor"), None),
        check_vma=False,
    )
```

```python
import functools
import itertools

import jax
import jax.numpy as jnp
import numpy as np
from jax import lax
from jax.experimental import pallas as pl
from jax.experimental.pallas import tpu as pltpu
from jax.sharding import PartitionSpec as P

BLOCK = 32
MIB = 2**20
VMEM = pl.BlockSpec(memory_space=pltpu.VMEM)
ANY = pl.BlockSpec(memory_space=pl.ANY)
GATHER_BYTES = (4 * MIB, 8 * MIB, 8 * MIB, 2 * MIB)
HADAMARD_BYTES = (0, 5 * MIB, 5 * MIB, 5 * MIB)


def walsh(order):
    index = np.arange(order)
    common = index[:, None] & index[None, :]
    parity = common * 0
    for shift in range(max(order.bit_length(), 1)):
        parity = parity ^ common >> shift & 1
    return (1 - 2 * parity).astype(np.float32)


def swapped(value, mask):
    pairs = [(source, source ^ mask) for source in range(lax.axis_size("tensor"))]
    return lax.ppermute(value, "tensor", pairs)


def in_hbm(value):
    return pltpu.with_memory_space_constraint(value, pltpu.HBM)


def in_vmem(value):
    return pltpu.with_memory_space_constraint(value, pltpu.VMEM)


def divisor(size, most, step):
    return max(d for d in range(step, min(size, most) + 1, step) if size % d == 0)


def fetch(weight, first, rows, after):
    def kernel(weight_ref, *refs):
        out_ref, sem = refs[-2:]
        copy = pltpu.make_async_copy(weight_ref.at[pl.ds(first, rows)], out_ref, sem)
        copy.start()
        copy.wait()

    width = weight.shape[1]
    size = rows * width * weight.dtype.itemsize
    return pl.pallas_call(
        kernel,
        out_shape=jax.ShapeDtypeStruct((rows, width), weight.dtype),
        in_specs=[ANY] * (1 + len(after)),
        out_specs=VMEM,
        scratch_shapes=[pltpu.SemaphoreType.DMA],
        cost_estimate=pl.CostEstimate(flops=0, transcendentals=0, bytes_accessed=2 * size),
        compiler_params=pltpu.CompilerParams(vmem_limit_bytes=MIB),
    )(in_hbm(weight), *after)


class Fetched:
    def __init__(self, weight, chunk, most):
        self.weight, self.chunk, self.most = weight, chunk, most
        self.rows, self.pieces = 0, []

    def beside(self, value, size, after):
        row = self.weight.shape[1] * self.weight.dtype.itemsize * self.chunk
        rows = min(size // row * self.chunk, self.most - self.rows)
        if rows <= 0:
            return value
        piece = fetch(self.weight, self.rows, rows, after)
        value, piece = lax.optimization_barrier((value, piece))
        self.rows += rows
        self.pieces.append(piece)
        return value


def gate_up(x, gate, up, fetched, chunk):
    tokens, depth = x.shape
    width = gate.shape[1]
    tile = divisor(width, 256, BLOCK)
    pieces = fetched.pieces
    count = len(pieces)
    chunks = [(0, first) for first in range(fetched.rows, depth, chunk)]
    chunks += [(1, first) for first in range(0, depth, chunk)]
    slots = min(8, len(chunks))
    spread = np.kron(np.eye(tile // BLOCK, dtype=np.float32), walsh(BLOCK))

    def kernel(x_ref, spread_ref, gate_ref, up_ref, *refs):
        piece_refs = refs[:count]
        out_ref, gate_acc, up_acc, buffer, sems = refs[count:]

        def copy(i):
            which, first = chunks[i]
            return pltpu.make_async_copy(
                (gate_ref, up_ref)[which].at[pl.ds(first, chunk)],
                buffer.at[i % slots],
                sems.at[i % slots],
            )

        for i in range(slots):
            copy(i).start()
        gate_acc[...] = jnp.zeros_like(gate_acc)
        up_acc[...] = jnp.zeros_like(up_acc)

        def add(acc, first, rows, ref):
            for n in range(0, width, tile):
                acc[:, n : n + tile] += jnp.dot(
                    x_ref[:, first : first + rows],
                    ref[:, n : n + tile],
                    preferred_element_type=jnp.float32,
                )

        first = 0
        for ref in piece_refs:
            add(gate_acc, first, ref.shape[0], ref)
            first += ref.shape[0]
        for i, (which, first) in enumerate(chunks):
            copy(i).wait()
            add((gate_acc, up_acc)[which], first, chunk, buffer.at[i % slots])
            if i + slots < len(chunks):
                copy(i + slots).start()
        for n in range(0, width, tile):
            hidden = jax.nn.silu(gate_acc[:, n : n + tile]) * up_acc[:, n : n + tile]
            coarse = hidden.astype(jnp.bfloat16)
            fine = (hidden - coarse.astype(jnp.float32)).astype(jnp.bfloat16)
            turned = jnp.dot(coarse, spread_ref[...], preferred_element_type=jnp.float32)
            turned += jnp.dot(fine, spread_ref[...], preferred_element_type=jnp.float32)
            out_ref[:, n : n + tile] = turned.astype(out_ref.dtype)

    size = gate.dtype.itemsize * width
    return pl.pallas_call(
        kernel,
        out_shape=jax.ShapeDtypeStruct((tokens, width), jnp.bfloat16),
        in_specs=[VMEM, VMEM, ANY, ANY] + [VMEM] * count,
        out_specs=VMEM,
        scratch_shapes=[
            pltpu.VMEM((tokens, width), jnp.float32),
            pltpu.VMEM((tokens, width), jnp.float32),
            pltpu.VMEM((slots, chunk, width), gate.dtype),
            pltpu.SemaphoreType.DMA((slots,)),
        ],
        cost_estimate=pl.CostEstimate(
            flops=4 * tokens * depth * width,
            transcendentals=tokens * width,
            bytes_accessed=len(chunks) * chunk * size,
        ),
        compiler_params=pltpu.CompilerParams(
            vmem_limit_bytes=slots * chunk * size + 3 * tokens * width * 4 + 4 * MIB
        ),
    )(
        x,
        jnp.asarray(spread, jnp.bfloat16),
        in_hbm(gate),
        in_hbm(up),
        *[in_vmem(piece) for piece in pieces],
    )


def down(rotated, weight, fetched, chunk):
    tokens, depth = rotated.shape
    width = weight.shape[1]
    tile = divisor(width, 256, 128)
    half = tokens // 2
    pieces = fetched.pieces
    count = len(pieces)
    chunks = list(range(fetched.rows, depth, chunk))

    def kernel(rotated_ref, weight_ref, *refs):
        piece_refs = refs[:count]
        keep_ref, send_ref, acc, buffer, sems = refs[count:]
        copies = [
            pltpu.make_async_copy(weight_ref.at[pl.ds(first, chunk)], buffer.at[i], sems.at[i])
            for i, first in enumerate(chunks)
        ]
        for copy in copies:
            copy.start()
        mine = lax.axis_index("tensor") % 2
        upper = mine == 1

        first = 0
        todo = []
        for ref in piece_refs:
            todo.append((first, ref.shape[0], ref, None))
            first += ref.shape[0]
        for i, first in enumerate(chunks):
            todo.append((first, chunk, buffer.at[i], copies[i]))
        for step, (first, rows, ref, copy) in enumerate(todo):
            if copy is not None:
                copy.wait()
            for n in range(0, width, tile):
                at = slice(n, n + tile)
                part = jnp.dot(
                    rotated_ref[:, first : first + rows],
                    ref[:, at],
                    preferred_element_type=jnp.float32,
                )
                if step:
                    part += acc[:, at]
                if step < len(todo) - 1:
                    acc[:, at] = part
                else:
                    low, high = part[:half], part[half:]
                    keep_ref[:, at] = jnp.where(upper, high, low)
                    send_ref[:, at] = jnp.where(upper, low, high).astype(send_ref.dtype)

    size = weight.dtype.itemsize * width
    return pl.pallas_call(
        kernel,
        out_shape=(
            jax.ShapeDtypeStruct((half, width), jnp.float32),
            jax.ShapeDtypeStruct((half, width), jnp.bfloat16),
        ),
        in_specs=[VMEM, ANY] + [VMEM] * count,
        out_specs=(VMEM, VMEM),
        scratch_shapes=[
            pltpu.VMEM((tokens, width), jnp.float32),
            pltpu.VMEM((len(chunks), chunk, width), weight.dtype),
            pltpu.SemaphoreType.DMA((len(chunks),)),
        ],
        cost_estimate=pl.CostEstimate(
            flops=2 * tokens * depth * width,
            transcendentals=0,
            bytes_accessed=len(chunks) * chunk * size,
        ),
        compiler_params=pltpu.CompilerParams(
            vmem_limit_bytes=len(chunks) * chunk * size + 2 * tokens * width * 4 + 4 * MIB
        ),
    )(rotated, in_hbm(weight), *[in_vmem(piece) for piece in pieces])


def masks_of(levels):
    return [
        (flips, sum(flip << level for flip, level in zip(flips, levels)))
        for flips in itertools.product((0, 1), repeat=len(levels))
    ]


def pick(choices, bits):
    if not bits:
        return choices[()]
    one, zero = (
        pick({k[1:]: v for k, v in choices.items() if k[0] == b}, bits[1:]) for b in (1, 0)
    )
    return jnp.where(bits[0], one, zero)


def xor(a, b):
    return tuple(i ^ j for i, j in zip(a, b))


def rounds_of(levels):
    return [(level,) for level in range(levels)[::-1]]


def per_device(tokens, gate_weight, up_weight, down_weight):
    devices = lax.axis_size("tensor")
    levels = devices.bit_length() - 1
    depth, width = gate_weight.shape
    scale = np.float32(1.0 / np.sqrt(devices * BLOCK))
    index = lax.axis_index("tensor")
    rounds = rounds_of(levels)
    upper = [(index >> level) & 1 == 1 for level in range(levels)]
    odd = {}
    for combined in rounds:
        for flips, mask in masks_of(combined[::-1]):
            odd[combined, flips] = functools.reduce(
                jnp.logical_xor,
                [upper[level] for flip, level in zip(flips, combined[::-1]) if not flip],
                jnp.zeros_like(upper[0]),
            )
    tokens, upper, odd = lax.optimization_barrier((tokens, upper, odd))

    gate_chunk = divisor(depth, 512, 16)
    gate_rows = Fetched(gate_weight, gate_chunk, depth - 2 * gate_chunk)
    piece = tokens
    for number, combined in enumerate(rounds):
        combined = combined[::-1]
        got = {(0,) * len(combined): piece}
        for flips, mask in masks_of(combined)[1:]:
            got[flips] = swapped(piece, mask)
        size = GATHER_BYTES[number] if number < len(GATHER_BYTES) else 0
        got[(0,) * len(combined)] = gate_rows.beside(piece, size, [piece] if number else [])
        bits = [upper[level] for level in combined]
        rows = []
        for slot in itertools.product((0, 1), repeat=len(combined)):
            rows.append(pick({xor(slot, flips): v for flips, v in got.items()}, bits))
        piece = jnp.concatenate(rows, axis=0)

    local = gate_up(piece, gate_weight, up_weight, gate_rows, gate_chunk)

    down_chunk = divisor(width, 256, 16)
    down_rows = Fetched(down_weight, down_chunk, width - down_chunk)
    for number, combined in enumerate(rounds[::-1]):
        levels_of = combined[::-1]
        last = number == len(rounds) - 1
        got = {}
        for flips, mask in masks_of(levels_of)[1:]:
            got[flips] = swapped(local, mask)
        size = HADAMARD_BYTES[number] if number < len(HADAMARD_BYTES) else 0
        got[(0,) * len(combined)] = down_rows.beside(local, size, [local])
        turned = 0.0
        for flips, value in got.items():
            value = value.astype(jnp.float32)
            if not all(flips):
                value = jnp.where(odd[combined, flips], -value, value)
            turned += value
        if last:
            turned *= scale
        local = turned.astype(jnp.bfloat16)

    keep, send = down(local, down_weight, down_rows, down_chunk)
    terms = keep + swapped(send, 1).astype(jnp.float32)
    for combined in rounds[::-1][1:]:
        combined = combined[::-1]
        parts = terms.reshape((2,) * len(combined) + (-1, terms.shape[1]))
        bits = [upper[level] for level in combined]
        total = None
        for flips, mask in masks_of(combined):
            slots = {
                xor(slot, flips): parts[slot]
                for slot in itertools.product((0, 1), repeat=len(combined))
            }
            part = pick(slots, bits)
            if mask:
                part = swapped(part.astype(jnp.bfloat16), mask).astype(jnp.float32)
            total = part if total is None else total + part
        terms = total
    return terms.astype(jnp.bfloat16)


def solution(mesh):
    return jax.shard_map(
        per_device,
        mesh=mesh,
        in_specs=(
            P(("groups", "tensor"), None),
            P(None, "tensor"),
            P(None, "tensor"),
            P("tensor", None),
        ),
        out_specs=P(("groups", "tensor"), None),
        check_vma=False,
    )
```

```python
import functools
import itertools

import jax
import jax.numpy as jnp
import numpy as np
from jax import lax
from jax.experimental import pallas as pl
from jax.experimental.pallas import tpu as pltpu
from jax.sharding import PartitionSpec as P

BLOCK = 32
MIB = 2**20
VMEM = pl.BlockSpec(memory_space=pltpu.VMEM)
ANY = pl.BlockSpec(memory_space=pl.ANY)
GATHER_BYTES = (4 * MIB, 12 * MIB, 0)
HADAMARD_BYTES = (0, 8 * MIB, 8 * MIB)


def walsh(order):
    index = np.arange(order)
    common = index[:, None] & index[None, :]
    parity = common * 0
    for shift in range(max(order.bit_length(), 1)):
        parity = parity ^ common >> shift & 1
    return (1 - 2 * parity).astype(np.float32)


def swapped(value, mask):
    pairs = [(source, source ^ mask) for source in range(lax.axis_size("tensor"))]
    return lax.ppermute(value, "tensor", pairs)


def in_hbm(value):
    return pltpu.with_memory_space_constraint(value, pltpu.HBM)


def in_vmem(value):
    return pltpu.with_memory_space_constraint(value, pltpu.VMEM)


def divisor(size, most, step):
    return max(d for d in range(step, min(size, most) + 1, step) if size % d == 0)


def fetch(weight, first, rows, after):
    def kernel(weight_ref, *refs):
        out_ref, sem = refs[-2:]
        copy = pltpu.make_async_copy(weight_ref.at[pl.ds(first, rows)], out_ref, sem)
        copy.start()
        copy.wait()

    width = weight.shape[1]
    size = rows * width * weight.dtype.itemsize
    return pl.pallas_call(
        kernel,
        out_shape=jax.ShapeDtypeStruct((rows, width), weight.dtype),
        in_specs=[ANY] * (1 + len(after)),
        out_specs=VMEM,
        scratch_shapes=[pltpu.SemaphoreType.DMA],
        cost_estimate=pl.CostEstimate(flops=0, transcendentals=0, bytes_accessed=2 * size),
        compiler_params=pltpu.CompilerParams(vmem_limit_bytes=MIB),
    )(in_hbm(weight), *after)


class Fetched:
    def __init__(self, weight, chunk, most):
        self.weight, self.chunk, self.most = weight, chunk, most
        self.rows, self.pieces = 0, []

    def beside(self, value, size, after):
        row = self.weight.shape[1] * self.weight.dtype.itemsize * self.chunk
        rows = min(size // row * self.chunk, self.most - self.rows)
        if rows <= 0:
            return value
        piece = fetch(self.weight, self.rows, rows, after)
        value, piece = lax.optimization_barrier((value, piece))
        self.rows += rows
        self.pieces.append(piece)
        return value


def gate_up(x, gate, up, fetched, chunk):
    tokens, depth = x.shape
    width = gate.shape[1]
    tile = divisor(width, 256, BLOCK)
    pieces = fetched.pieces
    count = len(pieces)
    chunks = [(0, first) for first in range(fetched.rows, depth, chunk)]
    chunks += [(1, first) for first in range(0, depth, chunk)]
    slots = min(8, len(chunks))
    spread = np.kron(np.eye(tile // BLOCK, dtype=np.float32), walsh(BLOCK))

    def kernel(x_ref, spread_ref, gate_ref, up_ref, *refs):
        piece_refs = refs[:count]
        out_ref, gate_acc, up_acc, buffer, sems = refs[count:]

        def copy(i):
            which, first = chunks[i]
            return pltpu.make_async_copy(
                (gate_ref, up_ref)[which].at[pl.ds(first, chunk)],
                buffer.at[i % slots],
                sems.at[i % slots],
            )

        for i in range(slots):
            copy(i).start()
        gate_acc[...] = jnp.zeros_like(gate_acc)
        up_acc[...] = jnp.zeros_like(up_acc)

        def add(acc, first, rows, ref):
            for k in range(0, rows, chunk):
                for n in range(0, width, tile):
                    acc[:, n : n + tile] += jnp.dot(
                        x_ref[:, first + k : first + k + chunk],
                        ref[k : k + chunk, n : n + tile],
                        preferred_element_type=jnp.float32,
                    )

        first = 0
        for ref in piece_refs:
            add(gate_acc, first, ref.shape[0], ref)
            first += ref.shape[0]
        for i, (which, first) in enumerate(chunks):
            copy(i).wait()
            add((gate_acc, up_acc)[which], first, chunk, buffer.at[i % slots])
            if i + slots < len(chunks):
                copy(i + slots).start()
        for n in range(0, width, tile):
            hidden = jax.nn.silu(gate_acc[:, n : n + tile]) * up_acc[:, n : n + tile]
            coarse = hidden.astype(jnp.bfloat16)
            fine = (hidden - coarse.astype(jnp.float32)).astype(jnp.bfloat16)
            turned = jnp.dot(coarse, spread_ref[...], preferred_element_type=jnp.float32)
            turned += jnp.dot(fine, spread_ref[...], preferred_element_type=jnp.float32)
            out_ref[:, n : n + tile] = turned.astype(out_ref.dtype)

    size = gate.dtype.itemsize * width
    return pl.pallas_call(
        kernel,
        out_shape=jax.ShapeDtypeStruct((tokens, width), jnp.bfloat16),
        in_specs=[VMEM, VMEM, ANY, ANY] + [VMEM] * count,
        out_specs=VMEM,
        scratch_shapes=[
            pltpu.VMEM((tokens, width), jnp.float32),
            pltpu.VMEM((tokens, width), jnp.float32),
            pltpu.VMEM((slots, chunk, width), gate.dtype),
            pltpu.SemaphoreType.DMA((slots,)),
        ],
        cost_estimate=pl.CostEstimate(
            flops=4 * tokens * depth * width,
            transcendentals=tokens * width,
            bytes_accessed=len(chunks) * chunk * size,
        ),
        compiler_params=pltpu.CompilerParams(
            vmem_limit_bytes=slots * chunk * size + 3 * tokens * width * 4 + 4 * MIB
        ),
    )(
        x,
        jnp.asarray(spread, jnp.bfloat16),
        in_hbm(gate),
        in_hbm(up),
        *[in_vmem(piece) for piece in pieces],
    )


def down(rotated, weight, fetched, chunk):
    tokens, depth = rotated.shape
    width = weight.shape[1]
    tile = divisor(width, 256, 128)
    half = tokens // 2
    pieces = fetched.pieces
    count = len(pieces)
    chunks = list(range(fetched.rows, depth, chunk))

    def kernel(rotated_ref, weight_ref, *refs):
        piece_refs = refs[:count]
        keep_ref, send_ref, acc, buffer, sems = refs[count:]
        copies = [
            pltpu.make_async_copy(weight_ref.at[pl.ds(first, chunk)], buffer.at[i], sems.at[i])
            for i, first in enumerate(chunks)
        ]
        for copy in copies:
            copy.start()
        mine = lax.axis_index("tensor") % 2
        upper = mine == 1

        first = 0
        todo = []
        for ref in piece_refs:
            todo.append((first, ref.shape[0], ref, None))
            first += ref.shape[0]
        for i, first in enumerate(chunks):
            todo.append((first, chunk, buffer.at[i], copies[i]))
        for step, (first, rows, ref, copy) in enumerate(todo):
            if copy is not None:
                copy.wait()
            for n in range(0, width, tile):
                at = slice(n, n + tile)
                part = jnp.dot(
                    rotated_ref[:, first : first + rows],
                    ref[:, at],
                    preferred_element_type=jnp.float32,
                )
                if step:
                    part += acc[:, at]
                if step < len(todo) - 1:
                    acc[:, at] = part
                else:
                    low, high = part[:half], part[half:]
                    keep_ref[:, at] = jnp.where(upper, high, low)
                    send_ref[:, at] = jnp.where(upper, low, high).astype(send_ref.dtype)

    size = weight.dtype.itemsize * width
    return pl.pallas_call(
        kernel,
        out_shape=(
            jax.ShapeDtypeStruct((half, width), jnp.float32),
            jax.ShapeDtypeStruct((half, width), jnp.bfloat16),
        ),
        in_specs=[VMEM, ANY] + [VMEM] * count,
        out_specs=(VMEM, VMEM),
        scratch_shapes=[
            pltpu.VMEM((tokens, width), jnp.float32),
            pltpu.VMEM((len(chunks), chunk, width), weight.dtype),
            pltpu.SemaphoreType.DMA((len(chunks),)),
        ],
        cost_estimate=pl.CostEstimate(
            flops=2 * tokens * depth * width,
            transcendentals=0,
            bytes_accessed=len(chunks) * chunk * size,
        ),
        compiler_params=pltpu.CompilerParams(
            vmem_limit_bytes=len(chunks) * chunk * size + 2 * tokens * width * 4 + 4 * MIB
        ),
    )(rotated, in_hbm(weight), *[in_vmem(piece) for piece in pieces])


def masks_of(levels):
    return [
        (flips, sum(flip << level for flip, level in zip(flips, levels)))
        for flips in itertools.product((0, 1), repeat=len(levels))
    ]


def pick(choices, bits):
    if not bits:
        return choices[()]
    one, zero = (
        pick({k[1:]: v for k, v in choices.items() if k[0] == b}, bits[1:]) for b in (1, 0)
    )
    return jnp.where(bits[0], one, zero)


def xor(a, b):
    return tuple(i ^ j for i, j in zip(a, b))


def gather_rounds(levels):
    return [(level,) for level in range(levels)[:2:-1]] + [(1, 2), (0,)]


def hadamard_rounds(levels):
    return [(0,)] + [(level,) for level in range(levels)[3:]] + [(2, 1)]


def per_device(tokens, gate_weight, up_weight, down_weight):
    devices = lax.axis_size("tensor")
    levels = devices.bit_length() - 1
    depth, width = gate_weight.shape
    scale = np.float32(1.0 / np.sqrt(devices * BLOCK))
    index = lax.axis_index("tensor")
    rounds = gather_rounds(levels)
    turns = hadamard_rounds(levels)
    upper = [(index >> level) & 1 == 1 for level in range(levels)]
    odd = {}
    for combined in turns:
        for flips, mask in masks_of(combined):
            odd[combined, flips] = functools.reduce(
                jnp.logical_xor,
                [upper[level] for flip, level in zip(flips, combined) if not flip],
                jnp.zeros_like(upper[0]),
            )
    tokens, upper, odd = lax.optimization_barrier((tokens, upper, odd))

    gate_chunk = divisor(depth, 512, 16)
    gate_rows = Fetched(gate_weight, gate_chunk, depth - 2 * gate_chunk)
    piece = tokens
    for number, combined in enumerate(rounds):
        combined = combined[::-1]
        got = {(0,) * len(combined): piece}
        for flips, mask in masks_of(combined)[1:]:
            got[flips] = swapped(piece, mask)
        size = GATHER_BYTES[number] if number < len(GATHER_BYTES) else 0
        got[(0,) * len(combined)] = gate_rows.beside(piece, size, [piece] if number else [])
        bits = [upper[level] for level in combined]
        rows = []
        for slot in itertools.product((0, 1), repeat=len(combined)):
            rows.append(pick({xor(slot, flips): v for flips, v in got.items()}, bits))
        piece = jnp.concatenate(rows, axis=0)

    local = gate_up(piece, gate_weight, up_weight, gate_rows, gate_chunk)

    down_chunk = divisor(width, 256, 16)
    down_rows = Fetched(down_weight, down_chunk, width - down_chunk)
    for number, combined in enumerate(turns):
        last = number == len(turns) - 1
        got = {}
        for flips, mask in masks_of(combined)[1:]:
            got[flips] = swapped(local, mask)
        size = HADAMARD_BYTES[number] if number < len(HADAMARD_BYTES) else 0
        got[(0,) * len(combined)] = down_rows.beside(local, size, [local])
        turned = 0.0
        for flips, value in got.items():
            value = value.astype(jnp.float32)
            if not all(flips):
                value = jnp.where(odd[combined, flips], -value, value)
            turned += value
        if last:
            turned *= scale
        local = turned.astype(jnp.bfloat16)

    keep, send = down(local, down_weight, down_rows, down_chunk)
    terms = keep + swapped(send, 1).astype(jnp.float32)
    for combined in rounds[::-1][1:]:
        combined = combined[::-1]
        parts = terms.reshape((2,) * len(combined) + (-1, terms.shape[1]))
        bits = [upper[level] for level in combined]
        total = None
        for flips, mask in masks_of(combined):
            slots = {
                xor(slot, flips): parts[slot]
                for slot in itertools.product((0, 1), repeat=len(combined))
            }
            part = pick(slots, bits)
            if mask:
                part = swapped(part.astype(jnp.bfloat16), mask).astype(jnp.float32)
            total = part if total is None else total + part
        terms = total
    return terms.astype(jnp.bfloat16)


def solution(mesh):
    return jax.shard_map(
        per_device,
        mesh=mesh,
        in_specs=(
            P(("groups", "tensor"), None),
            P(None, "tensor"),
            P(None, "tensor"),
            P("tensor", None),
        ),
        out_specs=P(("groups", "tensor"), None),
        check_vma=False,
    )
```

```python
import functools
import itertools

import jax
import jax.numpy as jnp
import numpy as np
from jax import lax
from jax.experimental import pallas as pl
from jax.experimental.pallas import tpu as pltpu
from jax.sharding import PartitionSpec as P

BLOCK = 32
MIB = 2**20
VMEM = pl.BlockSpec(memory_space=pltpu.VMEM)
ANY = pl.BlockSpec(memory_space=pl.ANY)
GATHER_BYTES = (4 * MIB, 12 * MIB, 3 * MIB)
HADAMARD_BYTES = (0, 12 * MIB, 12 * MIB)
SLOTS = 5


def walsh(order):
    index = np.arange(order)
    common = index[:, None] & index[None, :]
    parity = common * 0
    for shift in range(max(order.bit_length(), 1)):
        parity = parity ^ common >> shift & 1
    return (1 - 2 * parity).astype(np.float32)


def swapped(value, mask):
    pairs = [(source, source ^ mask) for source in range(lax.axis_size("tensor"))]
    return lax.ppermute(value, "tensor", pairs)


def in_hbm(value):
    return pltpu.with_memory_space_constraint(value, pltpu.HBM)


def in_vmem(value):
    return pltpu.with_memory_space_constraint(value, pltpu.VMEM)


def divisor(size, most, step):
    return max(d for d in range(step, min(size, most) + 1, step) if size % d == 0)


def fetch(weight, first, rows, after):
    def kernel(weight_ref, *refs):
        out_ref, sem = refs[-2:]
        copy = pltpu.make_async_copy(weight_ref.at[pl.ds(first, rows)], out_ref, sem)
        copy.start()
        copy.wait()

    width = weight.shape[1]
    size = rows * width * weight.dtype.itemsize
    return pl.pallas_call(
        kernel,
        out_shape=jax.ShapeDtypeStruct((rows, width), weight.dtype),
        in_specs=[ANY] * (1 + len(after)),
        out_specs=VMEM,
        scratch_shapes=[pltpu.SemaphoreType.DMA],
        cost_estimate=pl.CostEstimate(flops=0, transcendentals=0, bytes_accessed=2 * size),
        compiler_params=pltpu.CompilerParams(vmem_limit_bytes=MIB),
    )(in_hbm(weight), *after)


class Fetched:
    def __init__(self, weight, chunk, most):
        self.weight, self.chunk, self.most = weight, chunk, most
        self.rows, self.pieces = 0, []

    def beside(self, value, size, after):
        row = self.weight.shape[1] * self.weight.dtype.itemsize * self.chunk
        rows = min(size // row * self.chunk, self.most - self.rows)
        if rows <= 0:
            return value
        piece = fetch(self.weight, self.rows, rows, after)
        value, piece = lax.optimization_barrier((value, piece))
        self.rows += rows
        self.pieces.append(piece)
        return value


def gate_up(x, gate, up, fetched, chunk):
    tokens, depth = x.shape
    width = gate.shape[1]
    tile = divisor(width, 256, BLOCK)
    wide = width // 2 if width % 256 == 0 else tile
    pieces = fetched.pieces
    count = len(pieces)
    chunks = [
        (which, first, min(chunk, depth - first))
        for which, begin in ((0, fetched.rows), (1, 0))
        for first in range(begin, depth, chunk)
    ]
    slots = min(SLOTS, len(chunks))
    spread = np.kron(np.eye(tile // BLOCK, dtype=np.float32), walsh(BLOCK))

    def kernel(x_ref, spread_ref, gate_ref, up_ref, *refs):
        piece_refs = refs[:count]
        out_ref, gate_acc, up_acc, buffer, sems = refs[count:]

        def copy(i):
            which, first, rows = chunks[i]
            return pltpu.make_async_copy(
                (gate_ref, up_ref)[which].at[pl.ds(first, rows)],
                buffer.at[i % slots, pl.ds(0, rows)],
                sems.at[i % slots],
            )

        for i in range(slots):
            copy(i).start()
        gate_acc[...] = jnp.zeros_like(gate_acc)
        up_acc[...] = jnp.zeros_like(up_acc)

        def add(acc, first, rows, ref):
            for n in range(0, width, wide):
                acc[:, n : n + wide] += jnp.dot(
                    x_ref[:, first : first + rows],
                    ref[:rows, n : n + wide],
                    preferred_element_type=jnp.float32,
                )

        first = 0
        for ref in piece_refs:
            add(gate_acc, first, ref.shape[0], ref)
            first += ref.shape[0]
        for i, (which, first, rows) in enumerate(chunks):
            copy(i).wait()
            add((gate_acc, up_acc)[which], first, rows, buffer.at[i % slots])
            if i + slots < len(chunks):
                copy(i + slots).start()
        for n in range(0, width, tile):
            hidden = jax.nn.silu(gate_acc[:, n : n + tile]) * up_acc[:, n : n + tile]
            coarse = hidden.astype(jnp.bfloat16)
            fine = (hidden - coarse.astype(jnp.float32)).astype(jnp.bfloat16)
            turned = jnp.dot(coarse, spread_ref[...], preferred_element_type=jnp.float32)
            turned += jnp.dot(fine, spread_ref[...], preferred_element_type=jnp.float32)
            out_ref[:, n : n + tile] = turned.astype(out_ref.dtype)

    size = gate.dtype.itemsize * width
    return pl.pallas_call(
        kernel,
        out_shape=jax.ShapeDtypeStruct((tokens, width), jnp.bfloat16),
        in_specs=[VMEM, VMEM, ANY, ANY] + [VMEM] * count,
        out_specs=VMEM,
        scratch_shapes=[
            pltpu.VMEM((tokens, width), jnp.float32),
            pltpu.VMEM((tokens, width), jnp.float32),
            pltpu.VMEM((slots, chunk, width), gate.dtype),
            pltpu.SemaphoreType.DMA((slots,)),
        ],
        cost_estimate=pl.CostEstimate(
            flops=4 * tokens * depth * width,
            transcendentals=tokens * width,
            bytes_accessed=sum(rows for _, _, rows in chunks) * size,
        ),
        compiler_params=pltpu.CompilerParams(
            vmem_limit_bytes=slots * chunk * size + 3 * tokens * width * 4 + 4 * MIB
        ),
    )(
        x,
        jnp.asarray(spread, jnp.bfloat16),
        in_hbm(gate),
        in_hbm(up),
        *[in_vmem(piece) for piece in pieces],
    )


def down(rotated, weight, fetched, chunk):
    tokens, depth = rotated.shape
    width = weight.shape[1]
    tile = divisor(width, 256, 128)
    half = tokens // 2
    pieces = fetched.pieces
    count = len(pieces)
    chunks = list(range(fetched.rows, depth, chunk))

    def kernel(rotated_ref, weight_ref, *refs):
        piece_refs = refs[:count]
        keep_ref, send_ref, acc, buffer, sems = refs[count:]
        copies = [
            pltpu.make_async_copy(weight_ref.at[pl.ds(first, chunk)], buffer.at[i], sems.at[i])
            for i, first in enumerate(chunks)
        ]
        for copy in copies:
            copy.start()
        mine = lax.axis_index("tensor") % 2
        upper = mine == 1

        first = 0
        todo = []
        for ref in piece_refs:
            todo.append((first, ref.shape[0], ref, None))
            first += ref.shape[0]
        for i, first in enumerate(chunks):
            todo.append((first, chunk, buffer.at[i], copies[i]))
        for step, (first, rows, ref, copy) in enumerate(todo):
            if copy is not None:
                copy.wait()
            for n in range(0, width, tile):
                at = slice(n, n + tile)
                part = jnp.dot(
                    rotated_ref[:, first : first + rows],
                    ref[:, at],
                    preferred_element_type=jnp.float32,
                )
                if step:
                    part += acc[:, at]
                if step < len(todo) - 1:
                    acc[:, at] = part
                else:
                    low, high = part[:half], part[half:]
                    keep_ref[:, at] = jnp.where(upper, high, low)
                    send_ref[:, at] = jnp.where(upper, low, high).astype(send_ref.dtype)

    size = weight.dtype.itemsize * width
    return pl.pallas_call(
        kernel,
        out_shape=(
            jax.ShapeDtypeStruct((half, width), jnp.float32),
            jax.ShapeDtypeStruct((half, width), jnp.bfloat16),
        ),
        in_specs=[VMEM, ANY] + [VMEM] * count,
        out_specs=(VMEM, VMEM),
        scratch_shapes=[
            pltpu.VMEM((tokens, width), jnp.float32),
            pltpu.VMEM((len(chunks), chunk, width), weight.dtype),
            pltpu.SemaphoreType.DMA((len(chunks),)),
        ],
        cost_estimate=pl.CostEstimate(
            flops=2 * tokens * depth * width,
            transcendentals=0,
            bytes_accessed=len(chunks) * chunk * size,
        ),
        compiler_params=pltpu.CompilerParams(
            vmem_limit_bytes=len(chunks) * chunk * size + 2 * tokens * width * 4 + 4 * MIB
        ),
    )(rotated, in_hbm(weight), *[in_vmem(piece) for piece in pieces])


def masks_of(levels):
    return [
        (flips, sum(flip << level for flip, level in zip(flips, levels)))
        for flips in itertools.product((0, 1), repeat=len(levels))
    ]


def pick(choices, bits):
    if not bits:
        return choices[()]
    one, zero = (
        pick({k[1:]: v for k, v in choices.items() if k[0] == b}, bits[1:]) for b in (1, 0)
    )
    return jnp.where(bits[0], one, zero)


def xor(a, b):
    return tuple(i ^ j for i, j in zip(a, b))


def gather_rounds(levels):
    return [(level,) for level in range(levels)[:2:-1]] + [(1, 2), (0,)]


def hadamard_rounds(levels):
    return [(0,)] + [(level,) for level in range(levels)[3:]] + [(2, 1)]


def per_device(tokens, gate_weight, up_weight, down_weight):
    devices = lax.axis_size("tensor")
    levels = devices.bit_length() - 1
    depth, width = gate_weight.shape
    scale = np.float32(1.0 / np.sqrt(devices * BLOCK))
    index = lax.axis_index("tensor")
    rounds = gather_rounds(levels)
    turns = hadamard_rounds(levels)
    upper = [(index >> level) & 1 == 1 for level in range(levels)]
    odd = {}
    for combined in turns:
        for flips, mask in masks_of(combined):
            odd[combined, flips] = functools.reduce(
                jnp.logical_xor,
                [upper[level] for flip, level in zip(flips, combined) if not flip],
                jnp.zeros_like(upper[0]),
            )
    tokens, upper, odd = lax.optimization_barrier((tokens, upper, odd))

    gate_chunk = divisor(depth, 512, 16)
    gate_rows = Fetched(gate_weight, gate_chunk, depth - 2 * gate_chunk)
    piece = tokens
    for number, combined in enumerate(rounds):
        combined = combined[::-1]
        got = {(0,) * len(combined): piece}
        for flips, mask in masks_of(combined)[1:]:
            got[flips] = swapped(piece, mask)
        size = GATHER_BYTES[number] if number < len(GATHER_BYTES) else 0
        got[(0,) * len(combined)] = gate_rows.beside(piece, size, [piece] if number else [])
        bits = [upper[level] for level in combined]
        rows = []
        for slot in itertools.product((0, 1), repeat=len(combined)):
            rows.append(pick({xor(slot, flips): v for flips, v in got.items()}, bits))
        piece = jnp.concatenate(rows, axis=0)

    local = gate_up(piece, gate_weight, up_weight, gate_rows, 3 * gate_chunk)

    down_chunk = divisor(width, 256, 16)
    down_rows = Fetched(down_weight, down_chunk, width - down_chunk)
    for number, combined in enumerate(turns):
        last = number == len(turns) - 1
        got = {}
        for flips, mask in masks_of(combined)[1:]:
            got[flips] = swapped(local, mask)
        size = HADAMARD_BYTES[number] if number < len(HADAMARD_BYTES) else 0
        got[(0,) * len(combined)] = down_rows.beside(local, size, [local])
        turned = 0.0
        for flips, value in got.items():
            value = value.astype(jnp.float32)
            if not all(flips):
                value = jnp.where(odd[combined, flips], -value, value)
            turned += value
        if last:
            turned *= scale
        local = turned.astype(jnp.bfloat16)

    keep, send = down(local, down_weight, down_rows, down_chunk)
    terms = keep + swapped(send, 1).astype(jnp.float32)
    for combined in rounds[::-1][1:]:
        combined = combined[::-1]
        parts = terms.reshape((2,) * len(combined) + (-1, terms.shape[1]))
        bits = [upper[level] for level in combined]
        total = None
        for flips, mask in masks_of(combined):
            slots = {
                xor(slot, flips): parts[slot]
                for slot in itertools.product((0, 1), repeat=len(combined))
            }
            part = pick(slots, bits)
            if mask:
                part = swapped(part.astype(jnp.bfloat16), mask).astype(jnp.float32)
            total = part if total is None else total + part
        terms = total
    return terms.astype(jnp.bfloat16)


def solution(mesh):
    return jax.shard_map(
        per_device,
        mesh=mesh,
        in_specs=(
            P(("groups", "tensor"), None),
            P(None, "tensor"),
            P(None, "tensor"),
            P("tensor", None),
        ),
        out_specs=P(("groups", "tensor"), None),
        check_vma=False,
    )
```

```python
import functools
import itertools

import jax
import jax.numpy as jnp
import numpy as np
from jax import lax
from jax.experimental import pallas as pl
from jax.experimental.pallas import tpu as pltpu
from jax.sharding import PartitionSpec as P

BLOCK = 32
MIB = 2**20
VMEM = pl.BlockSpec(memory_space=pltpu.VMEM)
ANY = pl.BlockSpec(memory_space=pl.ANY)
GATHER_BYTES = (0 * MIB, 6 * MIB, 0 * MIB)
HADAMARD_BYTES = (0, 12 * MIB, 12 * MIB)
SLOTS = 4


def walsh(order):
    index = np.arange(order)
    common = index[:, None] & index[None, :]
    parity = common * 0
    for shift in range(max(order.bit_length(), 1)):
        parity = parity ^ common >> shift & 1
    return (1 - 2 * parity).astype(np.float32)


def swapped(value, mask):
    pairs = [(source, source ^ mask) for source in range(lax.axis_size("tensor"))]
    return lax.ppermute(value, "tensor", pairs)


def in_hbm(value):
    return pltpu.with_memory_space_constraint(value, pltpu.HBM)


def in_vmem(value):
    return pltpu.with_memory_space_constraint(value, pltpu.VMEM)


def divisor(size, most, step):
    return max(d for d in range(step, min(size, most) + 1, step) if size % d == 0)


def fetch(weight, first, rows, after):
    def kernel(weight_ref, *refs):
        out_ref, sem = refs[-2:]
        copy = pltpu.make_async_copy(weight_ref.at[pl.ds(first, rows)], out_ref, sem)
        copy.start()
        copy.wait()

    width = weight.shape[1]
    size = rows * width * weight.dtype.itemsize
    return pl.pallas_call(
        kernel,
        out_shape=jax.ShapeDtypeStruct((rows, width), weight.dtype),
        in_specs=[ANY] * (1 + len(after)),
        out_specs=VMEM,
        scratch_shapes=[pltpu.SemaphoreType.DMA],
        cost_estimate=pl.CostEstimate(flops=0, transcendentals=0, bytes_accessed=2 * size),
        compiler_params=pltpu.CompilerParams(vmem_limit_bytes=MIB),
    )(in_hbm(weight), *after)


class Fetched:
    def __init__(self, weight, chunk, most):
        self.weight, self.chunk, self.most = weight, chunk, most
        self.rows, self.pieces = 0, []

    def beside(self, value, size, after):
        row = self.weight.shape[1] * self.weight.dtype.itemsize * self.chunk
        rows = min(size // row * self.chunk, self.most - self.rows)
        if rows <= 0:
            return value
        piece = fetch(self.weight, self.rows, rows, after)
        value, piece = lax.optimization_barrier((value, piece))
        self.rows += rows
        self.pieces.append(piece)
        return value


def gate_up(x, gate, up, fetched, chunk):
    tokens, depth = x.shape
    width = gate.shape[1]
    tile = divisor(width, 256, BLOCK)
    wide = width // 2 if width % 256 == 0 else tile
    pieces = fetched.pieces
    count = len(pieces)
    chunks = [
        (which, first, min(chunk, depth - first))
        for which, begin in ((0, fetched.rows),)
        for first in range(begin, depth, chunk)
    ]
    slots = min(SLOTS, len(chunks))
    spread = np.kron(np.eye(tile // BLOCK, dtype=np.float32), walsh(BLOCK))

    def kernel(x_ref, spread_ref, gate_ref, up_ref, *refs):
        piece_refs = refs[:count]
        out_ref, gate_acc, up_acc, buffer, sems = refs[count:]

        def copy(i):
            which, first, rows = chunks[i]
            return pltpu.make_async_copy(
                (gate_ref, up_ref)[which].at[pl.ds(first, rows)],
                buffer.at[i % slots, pl.ds(0, rows)],
                sems.at[i % slots],
            )

        for i in range(slots):
            copy(i).start()
        gate_acc[...] = jnp.zeros_like(gate_acc)
        up_acc[...] = jnp.zeros_like(up_acc)

        def add(acc, first, rows, ref):
            for n in range(0, width, wide):
                acc[:, n : n + wide] += jnp.dot(
                    x_ref[:, first : first + rows],
                    ref[:rows, n : n + wide],
                    preferred_element_type=jnp.float32,
                )

        first = 0
        for ref in piece_refs:
            add(gate_acc, first, ref.shape[0], ref)
            first += ref.shape[0]
        add(up_acc, 0, depth, up_ref)
        for i, (which, first, rows) in enumerate(chunks):
            copy(i).wait()
            add((gate_acc, up_acc)[which], first, rows, buffer.at[i % slots])
            if i + slots < len(chunks):
                copy(i + slots).start()
        for n in range(0, width, tile):
            hidden = jax.nn.silu(gate_acc[:, n : n + tile]) * up_acc[:, n : n + tile]
            coarse = hidden.astype(jnp.bfloat16)
            fine = (hidden - coarse.astype(jnp.float32)).astype(jnp.bfloat16)
            turned = jnp.dot(coarse, spread_ref[...], preferred_element_type=jnp.float32)
            turned += jnp.dot(fine, spread_ref[...], preferred_element_type=jnp.float32)
            out_ref[:, n : n + tile] = turned.astype(out_ref.dtype)

    size = gate.dtype.itemsize * width
    return pl.pallas_call(
        kernel,
        out_shape=jax.ShapeDtypeStruct((tokens, width), jnp.bfloat16),
        in_specs=[VMEM, VMEM, ANY, VMEM] + [VMEM] * count,
        out_specs=VMEM,
        scratch_shapes=[
            pltpu.VMEM((tokens, width), jnp.float32),
            pltpu.VMEM((tokens, width), jnp.float32),
            pltpu.VMEM((slots, chunk, width), gate.dtype),
            pltpu.SemaphoreType.DMA((slots,)),
        ],
        cost_estimate=pl.CostEstimate(
            flops=4 * tokens * depth * width,
            transcendentals=tokens * width,
            bytes_accessed=sum(rows for _, _, rows in chunks) * size,
        ),
        compiler_params=pltpu.CompilerParams(
            vmem_limit_bytes=slots * chunk * size + 3 * tokens * width * 4 + 4 * MIB
        ),
    )(
        x,
        jnp.asarray(spread, jnp.bfloat16),
        in_hbm(gate),
        in_vmem(up),
        *[in_vmem(piece) for piece in pieces],
    )


def down(rotated, weight, fetched, chunk):
    tokens, depth = rotated.shape
    width = weight.shape[1]
    tile = divisor(width, 256, 128)
    half = tokens // 2
    pieces = fetched.pieces
    count = len(pieces)
    chunks = list(range(fetched.rows, depth, chunk))

    def kernel(rotated_ref, weight_ref, *refs):
        piece_refs = refs[:count]
        keep_ref, send_ref, acc, buffer, sems = refs[count:]
        copies = [
            pltpu.make_async_copy(weight_ref.at[pl.ds(first, chunk)], buffer.at[i], sems.at[i])
            for i, first in enumerate(chunks)
        ]
        for copy in copies:
            copy.start()
        mine = lax.axis_index("tensor") % 2
        upper = mine == 1

        first = 0
        todo = []
        for ref in piece_refs:
            todo.append((first, ref.shape[0], ref, None))
            first += ref.shape[0]
        for i, first in enumerate(chunks):
            todo.append((first, chunk, buffer.at[i], copies[i]))
        for step, (first, rows, ref, copy) in enumerate(todo):
            if copy is not None:
                copy.wait()
            for n in range(0, width, tile):
                at = slice(n, n + tile)
                part = jnp.dot(
                    rotated_ref[:, first : first + rows],
                    ref[:, at],
                    preferred_element_type=jnp.float32,
                )
                if step:
                    part += acc[:, at]
                if step < len(todo) - 1:
                    acc[:, at] = part
                else:
                    low, high = part[:half], part[half:]
                    keep_ref[:, at] = jnp.where(upper, high, low)
                    send_ref[:, at] = jnp.where(upper, low, high).astype(send_ref.dtype)

    size = weight.dtype.itemsize * width
    return pl.pallas_call(
        kernel,
        out_shape=(
            jax.ShapeDtypeStruct((half, width), jnp.float32),
            jax.ShapeDtypeStruct((half, width), jnp.bfloat16),
        ),
        in_specs=[VMEM, ANY] + [VMEM] * count,
        out_specs=(VMEM, VMEM),
        scratch_shapes=[
            pltpu.VMEM((tokens, width), jnp.float32),
            pltpu.VMEM((len(chunks), chunk, width), weight.dtype),
            pltpu.SemaphoreType.DMA((len(chunks),)),
        ],
        cost_estimate=pl.CostEstimate(
            flops=2 * tokens * depth * width,
            transcendentals=0,
            bytes_accessed=len(chunks) * chunk * size,
        ),
        compiler_params=pltpu.CompilerParams(
            vmem_limit_bytes=len(chunks) * chunk * size + 2 * tokens * width * 4 + 4 * MIB
        ),
    )(rotated, in_hbm(weight), *[in_vmem(piece) for piece in pieces])


def masks_of(levels):
    return [
        (flips, sum(flip << level for flip, level in zip(flips, levels)))
        for flips in itertools.product((0, 1), repeat=len(levels))
    ]


def pick(choices, bits):
    if not bits:
        return choices[()]
    one, zero = (
        pick({k[1:]: v for k, v in choices.items() if k[0] == b}, bits[1:]) for b in (1, 0)
    )
    return jnp.where(bits[0], one, zero)


def xor(a, b):
    return tuple(i ^ j for i, j in zip(a, b))


def gather_rounds(levels):
    return [(level,) for level in range(levels)[:2:-1]] + [(1, 2), (0,)]


def hadamard_rounds(levels):
    return [(0,)] + [(level,) for level in range(levels)[3:]] + [(2, 1)]


def per_device(tokens, gate_weight, up_weight, down_weight):
    devices = lax.axis_size("tensor")
    levels = devices.bit_length() - 1
    depth, width = gate_weight.shape
    scale = np.float32(1.0 / np.sqrt(devices * BLOCK))
    index = lax.axis_index("tensor")
    rounds = gather_rounds(levels)
    turns = hadamard_rounds(levels)
    upper = [(index >> level) & 1 == 1 for level in range(levels)]
    odd = {}
    for combined in turns:
        for flips, mask in masks_of(combined):
            odd[combined, flips] = functools.reduce(
                jnp.logical_xor,
                [upper[level] for flip, level in zip(flips, combined) if not flip],
                jnp.zeros_like(upper[0]),
            )
    tokens, upper, odd = lax.optimization_barrier((tokens, upper, odd))

    gate_chunk = divisor(depth, 512, 16)
    gate_rows = Fetched(gate_weight, gate_chunk, depth - 2 * gate_chunk)
    piece = tokens
    for number, combined in enumerate(rounds):
        combined = combined[::-1]
        got = {(0,) * len(combined): piece}
        for flips, mask in masks_of(combined)[1:]:
            got[flips] = swapped(piece, mask)
        size = GATHER_BYTES[number] if number < len(GATHER_BYTES) else 0
        got[(0,) * len(combined)] = gate_rows.beside(piece, size, [piece] if number else [])
        bits = [upper[level] for level in combined]
        rows = []
        for slot in itertools.product((0, 1), repeat=len(combined)):
            rows.append(pick({xor(slot, flips): v for flips, v in got.items()}, bits))
        piece = jnp.concatenate(rows, axis=0)

    local = gate_up(piece, gate_weight, up_weight, gate_rows, 2 * gate_chunk)

    down_chunk = divisor(width, 256, 16)
    down_rows = Fetched(down_weight, down_chunk, width - down_chunk)
    for number, combined in enumerate(turns):
        last = number == len(turns) - 1
        got = {}
        for flips, mask in masks_of(combined)[1:]:
            got[flips] = swapped(local, mask)
        size = HADAMARD_BYTES[number] if number < len(HADAMARD_BYTES) else 0
        got[(0,) * len(combined)] = down_rows.beside(local, size, [local])
        turned = 0.0
        for flips, value in got.items():
            value = value.astype(jnp.float32)
            if not all(flips):
                value = jnp.where(odd[combined, flips], -value, value)
            turned += value
        if last:
            turned *= scale
        local = turned.astype(jnp.bfloat16)

    keep, send = down(local, down_weight, down_rows, down_chunk)
    terms = keep + swapped(send, 1).astype(jnp.float32)
    for combined in rounds[::-1][1:]:
        combined = combined[::-1]
        parts = terms.reshape((2,) * len(combined) + (-1, terms.shape[1]))
        bits = [upper[level] for level in combined]
        total = None
        for flips, mask in masks_of(combined):
            slots = {
                xor(slot, flips): parts[slot]
                for slot in itertools.product((0, 1), repeat=len(combined))
            }
            part = pick(slots, bits)
            if mask:
                part = swapped(part.astype(jnp.bfloat16), mask).astype(jnp.float32)
            total = part if total is None else total + part
        terms = total
    return terms.astype(jnp.bfloat16)


def solution(mesh):
    return jax.shard_map(
        per_device,
        mesh=mesh,
        in_specs=(
            P(("groups", "tensor"), None),
            P(None, "tensor"),
            P(None, "tensor"),
            P("tensor", None),
        ),
        out_specs=P(("groups", "tensor"), None),
        check_vma=False,
    )
```

```python
import functools
import itertools

import jax
import jax.numpy as jnp
import numpy as np
from jax import lax
from jax.experimental import pallas as pl
from jax.experimental.pallas import tpu as pltpu
from jax.sharding import PartitionSpec as P

BLOCK = 32
MIB = 2**20
VMEM = pl.BlockSpec(memory_space=pltpu.VMEM)
ANY = pl.BlockSpec(memory_space=pl.ANY)
GATHER_BYTES = (0 * MIB, 6 * MIB, 0 * MIB)
HADAMARD_BYTES = (0, 12 * MIB, 12 * MIB)
SLOTS = 4


def walsh(order):
    index = np.arange(order)
    common = index[:, None] & index[None, :]
    parity = common * 0
    for shift in range(max(order.bit_length(), 1)):
        parity = parity ^ common >> shift & 1
    return (1 - 2 * parity).astype(np.float32)


def swapped(value, mask):
    pairs = [(source, source ^ mask) for source in range(lax.axis_size("tensor"))]
    return lax.ppermute(value, "tensor", pairs)


def in_hbm(value):
    return pltpu.with_memory_space_constraint(value, pltpu.HBM)


def in_vmem(value):
    return pltpu.with_memory_space_constraint(value, pltpu.VMEM)


def divisor(size, most, step):
    return max(d for d in range(step, min(size, most) + 1, step) if size % d == 0)


def fetch(weight, first, rows, after):
    def kernel(weight_ref, *refs):
        out_ref, sem = refs[-2:]
        copy = pltpu.make_async_copy(weight_ref.at[pl.ds(first, rows)], out_ref, sem)
        copy.start()
        copy.wait()

    width = weight.shape[1]
    size = rows * width * weight.dtype.itemsize
    return pl.pallas_call(
        kernel,
        out_shape=jax.ShapeDtypeStruct((rows, width), weight.dtype),
        in_specs=[ANY] * (1 + len(after)),
        out_specs=VMEM,
        scratch_shapes=[pltpu.SemaphoreType.DMA],
        cost_estimate=pl.CostEstimate(flops=0, transcendentals=0, bytes_accessed=2 * size),
        compiler_params=pltpu.CompilerParams(vmem_limit_bytes=MIB),
    )(in_hbm(weight), *after)


def in_place(value):
    def kernel(value_ref, out_ref):
        out_ref[...] = value_ref[...]

    return pl.pallas_call(
        kernel,
        out_shape=jax.ShapeDtypeStruct(value.shape, value.dtype),
        in_specs=[VMEM],
        out_specs=VMEM,
        cost_estimate=pl.CostEstimate(
            flops=0, transcendentals=0, bytes_accessed=2 * value.size * value.dtype.itemsize
        ),
        compiler_params=pltpu.CompilerParams(vmem_limit_bytes=MIB),
    )(value)


class Fetched:
    def __init__(self, weight, chunk, most):
        self.weight, self.chunk, self.most = weight, chunk, most
        self.rows, self.pieces = 0, []

    def beside(self, value, size, after):
        row = self.weight.shape[1] * self.weight.dtype.itemsize * self.chunk
        rows = min(size // row * self.chunk, self.most - self.rows)
        if rows <= 0:
            return value
        piece = fetch(self.weight, self.rows, rows, after)
        value, piece = lax.optimization_barrier((value, piece))
        self.rows += rows
        self.pieces.append(piece)
        return value


def gate_up(x, gate, up, fetched, chunk):
    tokens, depth = x.shape
    width = gate.shape[1]
    tile = divisor(width, 256, BLOCK)
    wide = width // 2 if width % 256 == 0 else tile
    pieces = fetched.pieces
    count = len(pieces)
    chunks = [
        (which, first, min(chunk, depth - first))
        for which, begin in ((0, fetched.rows),)
        for first in range(begin, depth, chunk)
    ]
    slots = min(SLOTS, len(chunks))
    spread = np.kron(np.eye(tile // BLOCK, dtype=np.float32), walsh(BLOCK))

    def kernel(x_ref, spread_ref, gate_ref, up_ref, *refs):
        piece_refs = refs[:count]
        out_ref, gate_acc, up_acc, buffer, sems = refs[count:]

        def copy(i):
            which, first, rows = chunks[i]
            return pltpu.make_async_copy(
                (gate_ref, up_ref)[which].at[pl.ds(first, rows)],
                buffer.at[i % slots, pl.ds(0, rows)],
                sems.at[i % slots],
            )

        for i in range(slots):
            copy(i).start()
        gate_acc[...] = jnp.zeros_like(gate_acc)
        up_acc[...] = jnp.zeros_like(up_acc)

        def add(acc, first, rows, ref):
            for n in range(0, width, wide):
                acc[:, n : n + wide] += jnp.dot(
                    x_ref[:, first : first + rows],
                    ref[:rows, n : n + wide],
                    preferred_element_type=jnp.float32,
                )

        first = 0
        for ref in piece_refs:
            add(gate_acc, first, ref.shape[0], ref)
            first += ref.shape[0]
        add(up_acc, 0, depth, up_ref)
        for i, (which, first, rows) in enumerate(chunks):
            copy(i).wait()
            add((gate_acc, up_acc)[which], first, rows, buffer.at[i % slots])
            if i + slots < len(chunks):
                copy(i + slots).start()
        for n in range(0, width, tile):
            hidden = jax.nn.silu(gate_acc[:, n : n + tile]) * up_acc[:, n : n + tile]
            coarse = hidden.astype(jnp.bfloat16)
            fine = (hidden - coarse.astype(jnp.float32)).astype(jnp.bfloat16)
            turned = jnp.dot(coarse, spread_ref[...], preferred_element_type=jnp.float32)
            turned += jnp.dot(fine, spread_ref[...], preferred_element_type=jnp.float32)
            out_ref[:, n : n + tile] = turned.astype(out_ref.dtype)

    size = gate.dtype.itemsize * width
    return pl.pallas_call(
        kernel,
        out_shape=jax.ShapeDtypeStruct((tokens, width), jnp.bfloat16),
        in_specs=[VMEM, VMEM, ANY, VMEM] + [VMEM] * count,
        out_specs=VMEM,
        scratch_shapes=[
            pltpu.VMEM((tokens, width), jnp.float32),
            pltpu.VMEM((tokens, width), jnp.float32),
            pltpu.VMEM((slots, chunk, width), gate.dtype),
            pltpu.SemaphoreType.DMA((slots,)),
        ],
        cost_estimate=pl.CostEstimate(
            flops=4 * tokens * depth * width,
            transcendentals=tokens * width,
            bytes_accessed=sum(rows for _, _, rows in chunks) * size,
        ),
        compiler_params=pltpu.CompilerParams(
            vmem_limit_bytes=slots * chunk * size + 3 * tokens * width * 4 + 4 * MIB
        ),
    )(
        x,
        jnp.asarray(spread, jnp.bfloat16),
        in_hbm(gate),
        in_vmem(up),
        *[in_vmem(piece) for piece in pieces],
    )


def down(rotated, weight, fetched, chunk):
    tokens, depth = rotated.shape
    width = weight.shape[1]
    tile = divisor(width, 256, 128)
    half = tokens // 2
    pieces = fetched.pieces
    count = len(pieces)
    chunks = list(range(fetched.rows, depth, chunk))

    def kernel(rotated_ref, weight_ref, *refs):
        piece_refs = refs[:count]
        keep_ref, send_ref, acc, buffer, sems = refs[count:]
        copies = [
            pltpu.make_async_copy(weight_ref.at[pl.ds(first, chunk)], buffer.at[i], sems.at[i])
            for i, first in enumerate(chunks)
        ]
        for copy in copies:
            copy.start()
        mine = lax.axis_index("tensor") % 2
        upper = mine == 1

        first = 0
        todo = []
        for ref in piece_refs:
            todo.append((first, ref.shape[0], ref, None))
            first += ref.shape[0]
        for i, first in enumerate(chunks):
            todo.append((first, chunk, buffer.at[i], copies[i]))
        for step, (first, rows, ref, copy) in enumerate(todo):
            if copy is not None:
                copy.wait()
            for n in range(0, width, tile):
                at = slice(n, n + tile)
                part = jnp.dot(
                    rotated_ref[:, first : first + rows],
                    ref[:, at],
                    preferred_element_type=jnp.float32,
                )
                if step:
                    part += acc[:, at]
                if step < len(todo) - 1:
                    acc[:, at] = part
                else:
                    low, high = part[:half], part[half:]
                    keep_ref[:, at] = jnp.where(upper, high, low)
                    send_ref[:, at] = jnp.where(upper, low, high).astype(send_ref.dtype)

    size = weight.dtype.itemsize * width
    return pl.pallas_call(
        kernel,
        out_shape=(
            jax.ShapeDtypeStruct((half, width), jnp.float32),
            jax.ShapeDtypeStruct((half, width), jnp.bfloat16),
        ),
        in_specs=[VMEM, ANY] + [VMEM] * count,
        out_specs=(VMEM, VMEM),
        scratch_shapes=[
            pltpu.VMEM((tokens, width), jnp.float32),
            pltpu.VMEM((len(chunks), chunk, width), weight.dtype),
            pltpu.SemaphoreType.DMA((len(chunks),)),
        ],
        cost_estimate=pl.CostEstimate(
            flops=2 * tokens * depth * width,
            transcendentals=0,
            bytes_accessed=len(chunks) * chunk * size,
        ),
        compiler_params=pltpu.CompilerParams(
            vmem_limit_bytes=len(chunks) * chunk * size + 2 * tokens * width * 4 + 4 * MIB
        ),
    )(rotated, in_hbm(weight), *[in_vmem(piece) for piece in pieces])


def masks_of(levels):
    return [
        (flips, sum(flip << level for flip, level in zip(flips, levels)))
        for flips in itertools.product((0, 1), repeat=len(levels))
    ]


def pick(choices, bits):
    if not bits:
        return choices[()]
    one, zero = (
        pick({k[1:]: v for k, v in choices.items() if k[0] == b}, bits[1:]) for b in (1, 0)
    )
    return jnp.where(bits[0], one, zero)


def xor(a, b):
    return tuple(i ^ j for i, j in zip(a, b))


def gather_rounds(levels):
    return [(level,) for level in range(levels)[:2:-1]] + [(1, 2), (0,)]


def hadamard_rounds(levels):
    return [(0,)] + [(level,) for level in range(levels)[3:]] + [(2, 1)]


def per_device(tokens, gate_weight, up_weight, down_weight):
    devices = lax.axis_size("tensor")
    levels = devices.bit_length() - 1
    depth, width = gate_weight.shape
    scale = np.float32(1.0 / np.sqrt(devices * BLOCK))
    index = lax.axis_index("tensor")
    rounds = gather_rounds(levels)
    turns = hadamard_rounds(levels)
    upper = [(index >> level) & 1 == 1 for level in range(levels)]
    odd = {}
    for combined in turns:
        for flips, mask in masks_of(combined):
            odd[combined, flips] = functools.reduce(
                jnp.logical_xor,
                [upper[level] for flip, level in zip(flips, combined) if not flip],
                jnp.zeros_like(upper[0]),
            )
    tokens, upper, odd = lax.optimization_barrier((tokens, upper, odd))

    gate_chunk = divisor(depth, 512, 16)
    gate_rows = Fetched(gate_weight, gate_chunk, depth - 2 * gate_chunk)
    piece = tokens
    for number, combined in enumerate(rounds):
        combined = combined[::-1]
        got = {(0,) * len(combined): piece}
        for flips, mask in masks_of(combined)[1:]:
            got[flips] = swapped(piece, mask)
        size = GATHER_BYTES[number] if number < len(GATHER_BYTES) else 0
        if not number:
            piece = in_place(piece)
        got[(0,) * len(combined)] = gate_rows.beside(piece, size, [piece] if number else [])
        bits = [upper[level] for level in combined]
        rows = []
        for slot in itertools.product((0, 1), repeat=len(combined)):
            rows.append(pick({xor(slot, flips): v for flips, v in got.items()}, bits))
        piece = jnp.concatenate(rows, axis=0)

    local = gate_up(piece, gate_weight, up_weight, gate_rows, 2 * gate_chunk)

    down_chunk = divisor(width, 256, 16)
    down_rows = Fetched(down_weight, down_chunk, width - down_chunk)
    for number, combined in enumerate(turns):
        last = number == len(turns) - 1
        got = {}
        for flips, mask in masks_of(combined)[1:]:
            got[flips] = swapped(local, mask)
        size = HADAMARD_BYTES[number] if number < len(HADAMARD_BYTES) else 0
        got[(0,) * len(combined)] = down_rows.beside(local, size, [local])
        turned = 0.0
        for flips, value in got.items():
            value = value.astype(jnp.float32)
            if not all(flips):
                value = jnp.where(odd[combined, flips], -value, value)
            turned += value
        if last:
            turned *= scale
        local = turned.astype(jnp.bfloat16)

    keep, send = down(local, down_weight, down_rows, down_chunk)
    terms = keep + swapped(send, 1).astype(jnp.float32)
    for combined in rounds[::-1][1:]:
        combined = combined[::-1]
        parts = terms.reshape((2,) * len(combined) + (-1, terms.shape[1]))
        bits = [upper[level] for level in combined]
        total = None
        for flips, mask in masks_of(combined):
            slots = {
                xor(slot, flips): parts[slot]
                for slot in itertools.product((0, 1), repeat=len(combined))
            }
            part = pick(slots, bits)
            if mask:
                part = swapped(part.astype(jnp.bfloat16), mask).astype(jnp.float32)
            total = part if total is None else total + part
        terms = total
    return terms.astype(jnp.bfloat16)


def solution(mesh):
    return jax.shard_map(
        per_device,
        mesh=mesh,
        in_specs=(
            P(("groups", "tensor"), None),
            P(None, "tensor"),
            P(None, "tensor"),
            P("tensor", None),
        ),
        out_specs=P(("groups", "tensor"), None),
        check_vma=False,
    )
```

```python
import functools
import itertools

import jax
import jax.numpy as jnp
import numpy as np
from jax import lax
from jax.experimental import pallas as pl
from jax.experimental.pallas import tpu as pltpu
from jax.sharding import PartitionSpec as P

BLOCK = 32
MIB = 2**20
VMEM = pl.BlockSpec(memory_space=pltpu.VMEM)
ANY = pl.BlockSpec(memory_space=pl.ANY)
GATHER_BYTES = (0 * MIB, 6 * MIB, 0 * MIB)
HADAMARD_BYTES = (0, 12 * MIB, 12 * MIB)
SLOTS = 4


def walsh(order):
    index = np.arange(order)
    common = index[:, None] & index[None, :]
    parity = common * 0
    for shift in range(max(order.bit_length(), 1)):
        parity = parity ^ common >> shift & 1
    return (1 - 2 * parity).astype(np.float32)


def swapped(value, mask):
    pairs = [(source, source ^ mask) for source in range(lax.axis_size("tensor"))]
    return lax.ppermute(value, "tensor", pairs)


def in_hbm(value):
    return pltpu.with_memory_space_constraint(value, pltpu.HBM)


def in_vmem(value):
    return pltpu.with_memory_space_constraint(value, pltpu.VMEM)


def divisor(size, most, step):
    return max(d for d in range(step, min(size, most) + 1, step) if size % d == 0)


def fetch(weight, first, rows, after):
    def kernel(weight_ref, *refs):
        out_ref, sem = refs[-2:]
        copy = pltpu.make_async_copy(weight_ref.at[pl.ds(first, rows)], out_ref, sem)
        copy.start()
        copy.wait()

    width = weight.shape[1]
    size = rows * width * weight.dtype.itemsize
    return pl.pallas_call(
        kernel,
        out_shape=jax.ShapeDtypeStruct((rows, width), weight.dtype),
        in_specs=[ANY] * (1 + len(after)),
        out_specs=VMEM,
        scratch_shapes=[pltpu.SemaphoreType.DMA],
        cost_estimate=pl.CostEstimate(flops=0, transcendentals=0, bytes_accessed=2 * size),
        compiler_params=pltpu.CompilerParams(vmem_limit_bytes=MIB),
    )(in_hbm(weight), *after)


def in_place(value):
    def kernel(value_ref, out_ref):
        out_ref[...] = value_ref[...]

    return pl.pallas_call(
        kernel,
        out_shape=jax.ShapeDtypeStruct(value.shape, value.dtype),
        in_specs=[VMEM],
        out_specs=VMEM,
        cost_estimate=pl.CostEstimate(
            flops=0, transcendentals=0, bytes_accessed=2 * value.size * value.dtype.itemsize
        ),
        compiler_params=pltpu.CompilerParams(vmem_limit_bytes=MIB),
    )(value)


class Fetched:
    def __init__(self, weight, chunk, most):
        self.weight, self.chunk, self.most = weight, chunk, most
        self.rows, self.pieces = 0, []

    def beside(self, value, size, after):
        row = self.weight.shape[1] * self.weight.dtype.itemsize * self.chunk
        rows = min(size // row * self.chunk, self.most - self.rows)
        if rows <= 0:
            return value
        piece = fetch(self.weight, self.rows, rows, after)
        value, piece = lax.optimization_barrier((value, piece))
        self.rows += rows
        self.pieces.append(piece)
        return value


def gate_up(x, gate, up, fetched, chunk):
    tokens, depth = x.shape
    width = gate.shape[1]
    tile = divisor(width, 256, BLOCK)
    wide = width // 2 if width % 256 == 0 else tile
    pieces = fetched.pieces
    count = len(pieces)
    chunks = [
        (which, first, min(chunk, depth - first))
        for which, begin in ((0, fetched.rows),)
        for first in range(begin, depth, chunk)
    ]
    slots = min(SLOTS, len(chunks))
    spread = np.kron(np.eye(tile // BLOCK, dtype=np.float32), walsh(BLOCK))

    def kernel(x_ref, spread_ref, gate_ref, up_ref, *refs):
        piece_refs = refs[:count]
        out_ref, gate_acc, up_acc, buffer, sems = refs[count:]

        def copy(i):
            which, first, rows = chunks[i]
            return pltpu.make_async_copy(
                (gate_ref, up_ref)[which].at[pl.ds(first, rows)],
                buffer.at[i % slots, pl.ds(0, rows)],
                sems.at[i % slots],
            )

        for i in range(slots):
            copy(i).start()
        gate_acc[...] = jnp.zeros_like(gate_acc)
        up_acc[...] = jnp.zeros_like(up_acc)

        def add(acc, first, rows, ref):
            for n in range(0, width, wide):
                acc[:, n : n + wide] += jnp.dot(
                    x_ref[:, first : first + rows],
                    ref[:rows, n : n + wide],
                    preferred_element_type=jnp.float32,
                )

        first = 0
        for ref in piece_refs:
            add(gate_acc, first, ref.shape[0], ref)
            first += ref.shape[0]
        add(up_acc, 0, depth, up_ref)
        for i, (which, first, rows) in enumerate(chunks):
            copy(i).wait()
            add((gate_acc, up_acc)[which], first, rows, buffer.at[i % slots])
            if i + slots < len(chunks):
                copy(i + slots).start()
        for n in range(0, width, tile):
            hidden = jax.nn.silu(gate_acc[:, n : n + tile]) * up_acc[:, n : n + tile]
            coarse = hidden.astype(jnp.bfloat16)
            fine = (hidden - coarse.astype(jnp.float32)).astype(jnp.bfloat16)
            turned = jnp.dot(coarse, spread_ref[...], preferred_element_type=jnp.float32)
            turned += jnp.dot(fine, spread_ref[...], preferred_element_type=jnp.float32)
            out_ref[:, n : n + tile] = turned.astype(out_ref.dtype)

    size = gate.dtype.itemsize * width
    return pl.pallas_call(
        kernel,
        out_shape=jax.ShapeDtypeStruct((tokens, width), jnp.bfloat16),
        in_specs=[VMEM, VMEM, ANY, VMEM] + [VMEM] * count,
        out_specs=VMEM,
        scratch_shapes=[
            pltpu.VMEM((tokens, width), jnp.float32),
            pltpu.VMEM((tokens, width), jnp.float32),
            pltpu.VMEM((slots, chunk, width), gate.dtype),
            pltpu.SemaphoreType.DMA((slots,)),
        ],
        cost_estimate=pl.CostEstimate(
            flops=4 * tokens * depth * width,
            transcendentals=tokens * width,
            bytes_accessed=sum(rows for _, _, rows in chunks) * size,
        ),
        compiler_params=pltpu.CompilerParams(
            vmem_limit_bytes=slots * chunk * size + 3 * tokens * width * 4 + 4 * MIB
        ),
    )(
        x,
        jnp.asarray(spread, jnp.bfloat16),
        in_hbm(gate),
        in_vmem(up),
        *[in_vmem(piece) for piece in pieces],
    )


def down(rotated, weight, fetched, chunk):
    tokens, depth = rotated.shape
    width = weight.shape[1]
    tile = divisor(width, 256, 128)
    half = tokens // 2
    pieces = fetched.pieces
    count = len(pieces)
    chunks = list(range(fetched.rows, depth, chunk))

    def kernel(rotated_ref, weight_ref, *refs):
        piece_refs = refs[:count]
        keep_ref, send_ref, acc, buffer, sems = refs[count:]
        copies = [
            pltpu.make_async_copy(weight_ref.at[pl.ds(first, chunk)], buffer.at[i], sems.at[i])
            for i, first in enumerate(chunks)
        ]
        for copy in copies:
            copy.start()
        mine = lax.axis_index("tensor") % 2
        upper = mine == 1

        first = 0
        todo = []
        for ref in piece_refs:
            todo.append((first, ref.shape[0], ref, None))
            first += ref.shape[0]
        for i, first in enumerate(chunks):
            todo.append((first, chunk, buffer.at[i], copies[i]))
        for step, (first, rows, ref, copy) in enumerate(todo):
            if copy is not None:
                copy.wait()
            for n in range(0, width, tile):
                at = slice(n, n + tile)
                part = jnp.dot(
                    rotated_ref[:, first : first + rows],
                    ref[:, at],
                    preferred_element_type=jnp.float32,
                )
                if step:
                    part += acc[:, at]
                if step < len(todo) - 1:
                    acc[:, at] = part
                else:
                    low, high = part[:half], part[half:]
                    keep_ref[:, at] = jnp.where(upper, high, low)
                    send_ref[:, at] = jnp.where(upper, low, high).astype(send_ref.dtype)

    size = weight.dtype.itemsize * width
    return pl.pallas_call(
        kernel,
        out_shape=(
            jax.ShapeDtypeStruct((half, width), jnp.float32),
            jax.ShapeDtypeStruct((half, width), jnp.bfloat16),
        ),
        in_specs=[VMEM, ANY] + [VMEM] * count,
        out_specs=(VMEM, VMEM),
        scratch_shapes=[
            pltpu.VMEM((tokens, width), jnp.float32),
            pltpu.VMEM((len(chunks), chunk, width), weight.dtype),
            pltpu.SemaphoreType.DMA((len(chunks),)),
        ],
        cost_estimate=pl.CostEstimate(
            flops=2 * tokens * depth * width,
            transcendentals=0,
            bytes_accessed=len(chunks) * chunk * size,
        ),
        compiler_params=pltpu.CompilerParams(
            vmem_limit_bytes=len(chunks) * chunk * size + 2 * tokens * width * 4 + 4 * MIB
        ),
    )(rotated, in_hbm(weight), *[in_vmem(piece) for piece in pieces])


def masks_of(levels):
    return [
        (flips, sum(flip << level for flip, level in zip(flips, levels)))
        for flips in itertools.product((0, 1), repeat=len(levels))
    ]


def pick(choices, bits):
    if not bits:
        return choices[()]
    one, zero = (
        pick({k[1:]: v for k, v in choices.items() if k[0] == b}, bits[1:]) for b in (1, 0)
    )
    return jnp.where(bits[0], one, zero)


def xor(a, b):
    return tuple(i ^ j for i, j in zip(a, b))


def gather_rounds(levels):
    return [(level,) for level in range(levels)[:2:-1]] + [(2, 1), (0,)]


def hadamard_rounds(levels):
    return [(0,)] + [(level,) for level in range(levels)[3:]] + [(1, 2)]


def per_device(tokens, gate_weight, up_weight, down_weight):
    devices = lax.axis_size("tensor")
    levels = devices.bit_length() - 1
    depth, width = gate_weight.shape
    scale = np.float32(1.0 / np.sqrt(devices * BLOCK))
    index = lax.axis_index("tensor")
    rounds = gather_rounds(levels)
    turns = hadamard_rounds(levels)
    upper = [(index >> level) & 1 == 1 for level in range(levels)]
    odd = {}
    for combined in turns:
        for flips, mask in masks_of(combined):
            odd[combined, flips] = functools.reduce(
                jnp.logical_xor,
                [upper[level] for flip, level in zip(flips, combined) if not flip],
                jnp.zeros_like(upper[0]),
            )
    tokens, upper, odd = lax.optimization_barrier((tokens, upper, odd))

    gate_chunk = divisor(depth, 512, 16)
    gate_rows = Fetched(gate_weight, gate_chunk, depth - 2 * gate_chunk)
    piece = tokens
    for number, combined in enumerate(rounds):
        combined = combined[::-1]
        got = {(0,) * len(combined): piece}
        for flips, mask in masks_of(combined)[1:]:
            got[flips] = swapped(piece, mask)
        size = GATHER_BYTES[number] if number < len(GATHER_BYTES) else 0
        if not number:
            piece = in_place(piece)
        got[(0,) * len(combined)] = gate_rows.beside(piece, size, [piece] if number else [])
        bits = [upper[level] for level in combined]
        rows = []
        for slot in itertools.product((0, 1), repeat=len(combined)):
            rows.append(pick({xor(slot, flips): v for flips, v in got.items()}, bits))
        piece = jnp.concatenate(rows, axis=0)

    local = gate_up(piece, gate_weight, up_weight, gate_rows, 2 * gate_chunk)

    down_chunk = divisor(width, 256, 16)
    down_rows = Fetched(down_weight, down_chunk, width - down_chunk)
    for number, combined in enumerate(turns):
        last = number == len(turns) - 1
        got = {}
        for flips, mask in masks_of(combined)[1:]:
            got[flips] = swapped(local, mask)
        size = HADAMARD_BYTES[number] if number < len(HADAMARD_BYTES) else 0
        got[(0,) * len(combined)] = down_rows.beside(local, size, [local])
        turned = 0.0
        for flips, value in got.items():
            value = value.astype(jnp.float32)
            if not all(flips):
                value = jnp.where(odd[combined, flips], -value, value)
            turned += value
        if last:
            turned *= scale
        local = turned.astype(jnp.bfloat16)

    keep, send = down(local, down_weight, down_rows, down_chunk)
    terms = keep + swapped(send, 1).astype(jnp.float32)
    for combined in rounds[::-1][1:]:
        combined = combined[::-1]
        parts = terms.reshape((2,) * len(combined) + (-1, terms.shape[1]))
        bits = [upper[level] for level in combined]
        total = None
        for flips, mask in masks_of(combined):
            slots = {
                xor(slot, flips): parts[slot]
                for slot in itertools.product((0, 1), repeat=len(combined))
            }
            part = pick(slots, bits)
            if mask:
                part = swapped(part.astype(jnp.bfloat16), mask).astype(jnp.float32)
            total = part if total is None else total + part
        terms = total
    return terms.astype(jnp.bfloat16)


def solution(mesh):
    return jax.shard_map(
        per_device,
        mesh=mesh,
        in_specs=(
            P(("groups", "tensor"), None),
            P(None, "tensor"),
            P(None, "tensor"),
            P("tensor", None),
        ),
        out_specs=P(("groups", "tensor"), None),
        check_vma=False,
    )
```

```python
import functools
import itertools

import jax
import jax.numpy as jnp
import numpy as np
from jax import lax
from jax.experimental import pallas as pl
from jax.experimental.pallas import tpu as pltpu
from jax.sharding import PartitionSpec as P

BLOCK = 32
MIB = 2**20
VMEM = pl.BlockSpec(memory_space=pltpu.VMEM)
ANY = pl.BlockSpec(memory_space=pl.ANY)
GATHER_BYTES = (0 * MIB, 6 * MIB, 0 * MIB)
HADAMARD_BYTES = (0, 12 * MIB, 12 * MIB)
SLOTS = 4


def walsh(order):
    index = np.arange(order)
    common = index[:, None] & index[None, :]
    parity = common * 0
    for shift in range(max(order.bit_length(), 1)):
        parity = parity ^ common >> shift & 1
    return (1 - 2 * parity).astype(np.float32)


def swapped(value, mask):
    pairs = [(source, source ^ mask) for source in range(lax.axis_size("tensor"))]
    return lax.ppermute(value, "tensor", pairs)


def in_hbm(value):
    return pltpu.with_memory_space_constraint(value, pltpu.HBM)


def in_vmem(value):
    return pltpu.with_memory_space_constraint(value, pltpu.VMEM)


def divisor(size, most, step):
    return max(d for d in range(step, min(size, most) + 1, step) if size % d == 0)


def fetch(weight, first, rows, after):
    def kernel(weight_ref, *refs):
        out_ref, sem = refs[-2:]
        copy = pltpu.make_async_copy(weight_ref.at[pl.ds(first, rows)], out_ref, sem)
        copy.start()
        copy.wait()

    width = weight.shape[1]
    size = rows * width * weight.dtype.itemsize
    return pl.pallas_call(
        kernel,
        out_shape=jax.ShapeDtypeStruct((rows, width), weight.dtype),
        in_specs=[ANY] * (1 + len(after)),
        out_specs=VMEM,
        scratch_shapes=[pltpu.SemaphoreType.DMA],
        cost_estimate=pl.CostEstimate(flops=0, transcendentals=0, bytes_accessed=2 * size),
        compiler_params=pltpu.CompilerParams(vmem_limit_bytes=MIB),
    )(in_hbm(weight), *after)


def in_place(value):
    def kernel(value_ref, out_ref):
        out_ref[...] = value_ref[...]

    return pl.pallas_call(
        kernel,
        out_shape=jax.ShapeDtypeStruct(value.shape, value.dtype),
        in_specs=[VMEM],
        out_specs=VMEM,
        cost_estimate=pl.CostEstimate(
            flops=0, transcendentals=0, bytes_accessed=2 * value.size * value.dtype.itemsize
        ),
        compiler_params=pltpu.CompilerParams(vmem_limit_bytes=MIB),
    )(value)


class Fetched:
    def __init__(self, weight, chunk, most):
        self.weight, self.chunk, self.most = weight, chunk, most
        self.rows, self.pieces = 0, []

    def beside(self, value, size, after):
        row = self.weight.shape[1] * self.weight.dtype.itemsize * self.chunk
        rows = min(size // row * self.chunk, self.most - self.rows)
        if rows <= 0:
            return value
        piece = fetch(self.weight, self.rows, rows, after)
        value, piece = lax.optimization_barrier((value, piece))
        self.rows += rows
        self.pieces.append(piece)
        return value


def gate_up(x, gate, up, fetched, chunk):
    tokens, depth = x.shape
    width = gate.shape[1]
    tile = divisor(width, 256, BLOCK)
    wide = width // 2 if width % 256 == 0 else tile
    pieces = fetched.pieces
    count = len(pieces)
    chunks = [
        (which, first, min(chunk, depth - first))
        for which, begin in ((0, fetched.rows),)
        for first in range(begin, depth, chunk)
    ]
    slots = min(SLOTS, len(chunks))
    spread = np.kron(np.eye(tile // BLOCK, dtype=np.float32), walsh(BLOCK))

    def kernel(x_ref, spread_ref, gate_ref, up_ref, *refs):
        piece_refs = refs[:count]
        out_ref, gate_acc, up_acc, buffer, sems = refs[count:]

        def copy(i):
            which, first, rows = chunks[i]
            return pltpu.make_async_copy(
                (gate_ref, up_ref)[which].at[pl.ds(first, rows)],
                buffer.at[i % slots, pl.ds(0, rows)],
                sems.at[i % slots],
            )

        for i in range(slots):
            copy(i).start()
        gate_acc[...] = jnp.zeros_like(gate_acc)
        up_acc[...] = jnp.zeros_like(up_acc)

        def add(acc, first, rows, ref):
            for n in range(0, width, wide):
                acc[:, n : n + wide] += jnp.dot(
                    x_ref[:, first : first + rows],
                    ref[:rows, n : n + wide],
                    preferred_element_type=jnp.float32,
                )

        first = 0
        for ref in piece_refs:
            add(gate_acc, first, ref.shape[0], ref)
            first += ref.shape[0]
        add(up_acc, 0, depth, up_ref)
        for i, (which, first, rows) in enumerate(chunks):
            copy(i).wait()
            add((gate_acc, up_acc)[which], first, rows, buffer.at[i % slots])
            if i + slots < len(chunks):
                copy(i + slots).start()
        for n in range(0, width, tile):
            hidden = jax.nn.silu(gate_acc[:, n : n + tile]) * up_acc[:, n : n + tile]
            coarse = hidden.astype(jnp.bfloat16)
            fine = (hidden - coarse.astype(jnp.float32)).astype(jnp.bfloat16)
            turned = jnp.dot(coarse, spread_ref[...], preferred_element_type=jnp.float32)
            turned += jnp.dot(fine, spread_ref[...], preferred_element_type=jnp.float32)
            out_ref[:, n : n + tile] = turned.astype(out_ref.dtype)

    size = gate.dtype.itemsize * width
    return pl.pallas_call(
        kernel,
        out_shape=jax.ShapeDtypeStruct((tokens, width), jnp.bfloat16),
        in_specs=[VMEM, VMEM, ANY, VMEM] + [VMEM] * count,
        out_specs=VMEM,
        scratch_shapes=[
            pltpu.VMEM((tokens, width), jnp.float32),
            pltpu.VMEM((tokens, width), jnp.float32),
            pltpu.VMEM((slots, chunk, width), gate.dtype),
            pltpu.SemaphoreType.DMA((slots,)),
        ],
        cost_estimate=pl.CostEstimate(
            flops=4 * tokens * depth * width,
            transcendentals=tokens * width,
            bytes_accessed=sum(rows for _, _, rows in chunks) * size,
        ),
        compiler_params=pltpu.CompilerParams(
            vmem_limit_bytes=slots * chunk * size + 3 * tokens * width * 4 + 4 * MIB
        ),
    )(
        x,
        jnp.asarray(spread, jnp.bfloat16),
        in_hbm(gate),
        in_vmem(up),
        *[in_vmem(piece) for piece in pieces],
    )


def down(rotated, weight, fetched, chunk):
    tokens, depth = rotated.shape
    width = weight.shape[1]
    tile = divisor(width, 256, 128)
    half = tokens // 2
    pieces = fetched.pieces
    count = len(pieces)
    chunks = list(range(fetched.rows, depth, chunk))

    def kernel(rotated_ref, weight_ref, *refs):
        piece_refs = refs[:count]
        keep_ref, send_ref, acc, buffer, sems = refs[count:]
        copies = [
            pltpu.make_async_copy(weight_ref.at[pl.ds(first, chunk)], buffer.at[i], sems.at[i])
            for i, first in enumerate(chunks)
        ]
        for copy in copies:
            copy.start()
        mine = lax.axis_index("tensor") % 2
        upper = mine == 1

        first = 0
        todo = []
        for ref in piece_refs:
            todo.append((first, ref.shape[0], ref, None))
            first += ref.shape[0]
        for i, first in enumerate(chunks):
            todo.append((first, chunk, buffer.at[i], copies[i]))
        for step, (first, rows, ref, copy) in enumerate(todo):
            if copy is not None:
                copy.wait()
            for n in range(0, width, tile):
                at = slice(n, n + tile)
                part = jnp.dot(
                    rotated_ref[:, first : first + rows],
                    ref[:, at],
                    preferred_element_type=jnp.float32,
                )
                if step:
                    part += acc[:, at]
                if step < len(todo) - 1:
                    acc[:, at] = part
                else:
                    low, high = part[:half], part[half:]
                    keep_ref[:, at] = jnp.where(upper, high, low)
                    send_ref[:, at] = jnp.where(upper, low, high).astype(send_ref.dtype)

    size = weight.dtype.itemsize * width
    return pl.pallas_call(
        kernel,
        out_shape=(
            jax.ShapeDtypeStruct((half, width), jnp.float32),
            jax.ShapeDtypeStruct((half, width), jnp.bfloat16),
        ),
        in_specs=[VMEM, ANY] + [VMEM] * count,
        out_specs=(VMEM, VMEM),
        scratch_shapes=[
            pltpu.VMEM((tokens, width), jnp.float32),
            pltpu.VMEM((len(chunks), chunk, width), weight.dtype),
            pltpu.SemaphoreType.DMA((len(chunks),)),
        ],
        cost_estimate=pl.CostEstimate(
            flops=2 * tokens * depth * width,
            transcendentals=0,
            bytes_accessed=len(chunks) * chunk * size,
        ),
        compiler_params=pltpu.CompilerParams(
            vmem_limit_bytes=len(chunks) * chunk * size + 2 * tokens * width * 4 + 4 * MIB
        ),
    )(rotated, in_hbm(weight), *[in_vmem(piece) for piece in pieces])


def masks_of(levels):
    return [
        (flips, sum(flip << level for flip, level in zip(flips, levels)))
        for flips in itertools.product((0, 1), repeat=len(levels))
    ]


def pick(choices, bits):
    if not bits:
        return choices[()]
    one, zero = (
        pick({k[1:]: v for k, v in choices.items() if k[0] == b}, bits[1:]) for b in (1, 0)
    )
    return jnp.where(bits[0], one, zero)


def xor(a, b):
    return tuple(i ^ j for i, j in zip(a, b))


def gather_rounds(levels):
    return [(level,) for level in range(levels)[:2:-1]] + [(2, 1), (0,)]


def hadamard_rounds(levels):
    return [(0,), (1, 2)] + [(level,) for level in range(levels)[3:]]


def per_device(tokens, gate_weight, up_weight, down_weight):
    devices = lax.axis_size("tensor")
    levels = devices.bit_length() - 1
    depth, width = gate_weight.shape
    scale = np.float32(1.0 / np.sqrt(devices * BLOCK))
    index = lax.axis_index("tensor")
    rounds = gather_rounds(levels)
    turns = hadamard_rounds(levels)
    upper = [(index >> level) & 1 == 1 for level in range(levels)]
    odd = {}
    for combined in turns:
        for flips, mask in masks_of(combined):
            odd[combined, flips] = functools.reduce(
                jnp.logical_xor,
                [upper[level] for flip, level in zip(flips, combined) if not flip],
                jnp.zeros_like(upper[0]),
            )
    tokens, upper, odd = lax.optimization_barrier((tokens, upper, odd))

    gate_chunk = divisor(depth, 512, 16)
    gate_rows = Fetched(gate_weight, gate_chunk, depth - 2 * gate_chunk)
    piece = tokens
    for number, combined in enumerate(rounds):
        combined = combined[::-1]
        got = {(0,) * len(combined): piece}
        for flips, mask in masks_of(combined)[1:]:
            got[flips] = swapped(piece, mask)
        size = GATHER_BYTES[number] if number < len(GATHER_BYTES) else 0
        if not number:
            piece = in_place(piece)
        got[(0,) * len(combined)] = gate_rows.beside(piece, size, [piece] if number else [])
        bits = [upper[level] for level in combined]
        rows = []
        for slot in itertools.product((0, 1), repeat=len(combined)):
            rows.append(pick({xor(slot, flips): v for flips, v in got.items()}, bits))
        piece = jnp.concatenate(rows, axis=0)

    local = gate_up(piece, gate_weight, up_weight, gate_rows, 2 * gate_chunk)

    down_chunk = divisor(width, 256, 16)
    down_rows = Fetched(down_weight, down_chunk, width - down_chunk)
    for number, combined in enumerate(turns):
        last = number == len(turns) - 1
        got = {}
        for flips, mask in masks_of(combined)[1:]:
            got[flips] = swapped(local, mask)
        size = HADAMARD_BYTES[number] if number < len(HADAMARD_BYTES) else 0
        got[(0,) * len(combined)] = down_rows.beside(local, size, [local])
        turned = 0.0
        for flips, value in got.items():
            value = value.astype(jnp.float32)
            if not all(flips):
                value = jnp.where(odd[combined, flips], -value, value)
            turned += value
        if last:
            turned *= scale
        local = turned.astype(jnp.bfloat16)

    keep, send = down(local, down_weight, down_rows, down_chunk)
    terms = keep + swapped(send, 1).astype(jnp.float32)
    for combined in rounds[::-1][1:]:
        combined = combined[::-1]
        parts = terms.reshape((2,) * len(combined) + (-1, terms.shape[1]))
        bits = [upper[level] for level in combined]
        total = None
        for flips, mask in masks_of(combined):
            slots = {
                xor(slot, flips): parts[slot]
                for slot in itertools.product((0, 1), repeat=len(combined))
            }
            part = pick(slots, bits)
            if mask:
                part = swapped(part.astype(jnp.bfloat16), mask).astype(jnp.float32)
            total = part if total is None else total + part
        terms = total
    return terms.astype(jnp.bfloat16)


def solution(mesh):
    return jax.shard_map(
        per_device,
        mesh=mesh,
        in_specs=(
            P(("groups", "tensor"), None),
            P(None, "tensor"),
            P(None, "tensor"),
            P("tensor", None),
        ),
        out_specs=P(("groups", "tensor"), None),
        check_vma=False,
    )
```

```python
import functools
import itertools

import jax
import jax.numpy as jnp
import numpy as np
from jax import lax
from jax.experimental import pallas as pl
from jax.experimental.pallas import tpu as pltpu
from jax.sharding import PartitionSpec as P

BLOCK = 32
MIB = 2**20
VMEM = pl.BlockSpec(memory_space=pltpu.VMEM)
ANY = pl.BlockSpec(memory_space=pl.ANY)
GATHER_BYTES = (0 * MIB, 6 * MIB, 0 * MIB)
HADAMARD_BYTES = (0, 16 * MIB, 8 * MIB)
SLOTS = 4


def walsh(order):
    index = np.arange(order)
    common = index[:, None] & index[None, :]
    parity = common * 0
    for shift in range(max(order.bit_length(), 1)):
        parity = parity ^ common >> shift & 1
    return (1 - 2 * parity).astype(np.float32)


def swapped(value, mask):
    pairs = [(source, source ^ mask) for source in range(lax.axis_size("tensor"))]
    return lax.ppermute(value, "tensor", pairs)


def in_hbm(value):
    return pltpu.with_memory_space_constraint(value, pltpu.HBM)


def in_vmem(value):
    return pltpu.with_memory_space_constraint(value, pltpu.VMEM)


def divisor(size, most, step):
    return max(d for d in range(step, min(size, most) + 1, step) if size % d == 0)


def fetch(weight, first, rows, after):
    def kernel(weight_ref, *refs):
        out_ref, sem = refs[-2:]
        copy = pltpu.make_async_copy(weight_ref.at[pl.ds(first, rows)], out_ref, sem)
        copy.start()
        copy.wait()

    width = weight.shape[1]
    size = rows * width * weight.dtype.itemsize
    return pl.pallas_call(
        kernel,
        out_shape=jax.ShapeDtypeStruct((rows, width), weight.dtype),
        in_specs=[ANY] * (1 + len(after)),
        out_specs=VMEM,
        scratch_shapes=[pltpu.SemaphoreType.DMA],
        cost_estimate=pl.CostEstimate(flops=0, transcendentals=0, bytes_accessed=2 * size),
        compiler_params=pltpu.CompilerParams(vmem_limit_bytes=MIB),
    )(in_hbm(weight), *after)


def in_place(value):
    def kernel(value_ref, out_ref):
        out_ref[...] = value_ref[...]

    return pl.pallas_call(
        kernel,
        out_shape=jax.ShapeDtypeStruct(value.shape, value.dtype),
        in_specs=[VMEM],
        out_specs=VMEM,
        cost_estimate=pl.CostEstimate(
            flops=0, transcendentals=0, bytes_accessed=2 * value.size * value.dtype.itemsize
        ),
        compiler_params=pltpu.CompilerParams(vmem_limit_bytes=MIB),
    )(value)


class Fetched:
    def __init__(self, weight, chunk, most):
        self.weight, self.chunk, self.most = weight, chunk, most
        self.rows, self.pieces = 0, []

    def beside(self, value, size, after):
        row = self.weight.shape[1] * self.weight.dtype.itemsize * self.chunk
        rows = min(size // row * self.chunk, self.most - self.rows)
        if rows <= 0:
            return value
        piece = fetch(self.weight, self.rows, rows, after)
        value, piece = lax.optimization_barrier((value, piece))
        self.rows += rows
        self.pieces.append(piece)
        return value


def gate_up(x, gate, up, fetched, chunk):
    tokens, depth = x.shape
    width = gate.shape[1]
    tile = divisor(width, 256, BLOCK)
    wide = width // 2 if width % 256 == 0 else tile
    pieces = fetched.pieces
    count = len(pieces)
    chunks = [
        (which, first, min(chunk, depth - first))
        for which, begin in ((0, fetched.rows),)
        for first in range(begin, depth, chunk)
    ]
    slots = min(SLOTS, len(chunks))
    spread = np.kron(np.eye(tile // BLOCK, dtype=np.float32), walsh(BLOCK))

    def kernel(x_ref, spread_ref, gate_ref, up_ref, *refs):
        piece_refs = refs[:count]
        out_ref, gate_acc, up_acc, buffer, sems = refs[count:]

        def copy(i):
            which, first, rows = chunks[i]
            return pltpu.make_async_copy(
                (gate_ref, up_ref)[which].at[pl.ds(first, rows)],
                buffer.at[i % slots, pl.ds(0, rows)],
                sems.at[i % slots],
            )

        for i in range(slots):
            copy(i).start()
        gate_acc[...] = jnp.zeros_like(gate_acc)
        up_acc[...] = jnp.zeros_like(up_acc)

        def add(acc, first, rows, ref):
            for n in range(0, width, wide):
                acc[:, n : n + wide] += jnp.dot(
                    x_ref[:, first : first + rows],
                    ref[:rows, n : n + wide],
                    preferred_element_type=jnp.float32,
                )

        first = 0
        for ref in piece_refs:
            add(gate_acc, first, ref.shape[0], ref)
            first += ref.shape[0]
        add(up_acc, 0, depth, up_ref)
        for i, (which, first, rows) in enumerate(chunks):
            copy(i).wait()
            add((gate_acc, up_acc)[which], first, rows, buffer.at[i % slots])
            if i + slots < len(chunks):
                copy(i + slots).start()
        for n in range(0, width, tile):
            hidden = jax.nn.silu(gate_acc[:, n : n + tile]) * up_acc[:, n : n + tile]
            coarse = hidden.astype(jnp.bfloat16)
            fine = (hidden - coarse.astype(jnp.float32)).astype(jnp.bfloat16)
            turned = jnp.dot(coarse, spread_ref[...], preferred_element_type=jnp.float32)
            turned += jnp.dot(fine, spread_ref[...], preferred_element_type=jnp.float32)
            out_ref[:, n : n + tile] = turned.astype(out_ref.dtype)

    size = gate.dtype.itemsize * width
    return pl.pallas_call(
        kernel,
        out_shape=jax.ShapeDtypeStruct((tokens, width), jnp.bfloat16),
        in_specs=[VMEM, VMEM, ANY, VMEM] + [VMEM] * count,
        out_specs=VMEM,
        scratch_shapes=[
            pltpu.VMEM((tokens, width), jnp.float32),
            pltpu.VMEM((tokens, width), jnp.float32),
            pltpu.VMEM((slots, chunk, width), gate.dtype),
            pltpu.SemaphoreType.DMA((slots,)),
        ],
        cost_estimate=pl.CostEstimate(
            flops=4 * tokens * depth * width,
            transcendentals=tokens * width,
            bytes_accessed=sum(rows for _, _, rows in chunks) * size,
        ),
        compiler_params=pltpu.CompilerParams(
            vmem_limit_bytes=slots * chunk * size + 3 * tokens * width * 4 + 4 * MIB
        ),
    )(
        x,
        jnp.asarray(spread, jnp.bfloat16),
        in_hbm(gate),
        in_vmem(up),
        *[in_vmem(piece) for piece in pieces],
    )


def down(rotated, weight, fetched, chunk):
    tokens, depth = rotated.shape
    width = weight.shape[1]
    tile = divisor(width, 256, 128)
    half = tokens // 2
    pieces = fetched.pieces
    count = len(pieces)
    chunks = list(range(fetched.rows, depth, chunk))

    def kernel(rotated_ref, weight_ref, *refs):
        piece_refs = refs[:count]
        keep_ref, send_ref, acc, buffer, sems = refs[count:]
        copies = [
            pltpu.make_async_copy(weight_ref.at[pl.ds(first, chunk)], buffer.at[i], sems.at[i])
            for i, first in enumerate(chunks)
        ]
        for copy in copies:
            copy.start()
        mine = lax.axis_index("tensor") % 2
        upper = mine == 1

        first = 0
        todo = []
        for ref in piece_refs:
            todo.append((first, ref.shape[0], ref, None))
            first += ref.shape[0]
        for i, first in enumerate(chunks):
            todo.append((first, chunk, buffer.at[i], copies[i]))
        for step, (first, rows, ref, copy) in enumerate(todo):
            if copy is not None:
                copy.wait()
            for n in range(0, width, tile):
                at = slice(n, n + tile)
                part = jnp.dot(
                    rotated_ref[:, first : first + rows],
                    ref[:, at],
                    preferred_element_type=jnp.float32,
                )
                if step:
                    part += acc[:, at]
                if step < len(todo) - 1:
                    acc[:, at] = part
                else:
                    low, high = part[:half], part[half:]
                    keep_ref[:, at] = jnp.where(upper, high, low)
                    send_ref[:, at] = jnp.where(upper, low, high).astype(send_ref.dtype)

    size = weight.dtype.itemsize * width
    return pl.pallas_call(
        kernel,
        out_shape=(
            jax.ShapeDtypeStruct((half, width), jnp.float32),
            jax.ShapeDtypeStruct((half, width), jnp.bfloat16),
        ),
        in_specs=[VMEM, ANY] + [VMEM] * count,
        out_specs=(VMEM, VMEM),
        scratch_shapes=[
            pltpu.VMEM((tokens, width), jnp.float32),
            pltpu.VMEM((len(chunks), chunk, width), weight.dtype),
            pltpu.SemaphoreType.DMA((len(chunks),)),
        ],
        cost_estimate=pl.CostEstimate(
            flops=2 * tokens * depth * width,
            transcendentals=0,
            bytes_accessed=len(chunks) * chunk * size,
        ),
        compiler_params=pltpu.CompilerParams(
            vmem_limit_bytes=len(chunks) * chunk * size + 2 * tokens * width * 4 + 4 * MIB
        ),
    )(rotated, in_hbm(weight), *[in_vmem(piece) for piece in pieces])


def masks_of(levels):
    return [
        (flips, sum(flip << level for flip, level in zip(flips, levels)))
        for flips in itertools.product((0, 1), repeat=len(levels))
    ]


def pick(choices, bits):
    if not bits:
        return choices[()]
    one, zero = (
        pick({k[1:]: v for k, v in choices.items() if k[0] == b}, bits[1:]) for b in (1, 0)
    )
    return jnp.where(bits[0], one, zero)


def xor(a, b):
    return tuple(i ^ j for i, j in zip(a, b))


def gather_rounds(levels):
    return [(level,) for level in range(levels)[:2:-1]] + [(2, 1), (0,)]


def hadamard_rounds(levels):
    return [(0,)] + [(level,) for level in range(levels)[3:]] + [(1, 2)]


def per_device(tokens, gate_weight, up_weight, down_weight):
    devices = lax.axis_size("tensor")
    levels = devices.bit_length() - 1
    depth, width = gate_weight.shape
    scale = np.float32(1.0 / np.sqrt(devices * BLOCK))
    index = lax.axis_index("tensor")
    rounds = gather_rounds(levels)
    turns = hadamard_rounds(levels)
    upper = [(index >> level) & 1 == 1 for level in range(levels)]
    odd = {}
    for combined in turns:
        for flips, mask in masks_of(combined):
            odd[combined, flips] = functools.reduce(
                jnp.logical_xor,
                [upper[level] for flip, level in zip(flips, combined) if not flip],
                jnp.zeros_like(upper[0]),
            )
    tokens, upper, odd = lax.optimization_barrier((tokens, upper, odd))

    gate_chunk = divisor(depth, 512, 16)
    gate_rows = Fetched(gate_weight, gate_chunk, depth - 2 * gate_chunk)
    piece = tokens
    for number, combined in enumerate(rounds):
        combined = combined[::-1]
        got = {(0,) * len(combined): piece}
        for flips, mask in masks_of(combined)[1:]:
            got[flips] = swapped(piece, mask)
        size = GATHER_BYTES[number] if number < len(GATHER_BYTES) else 0
        if not number:
            piece = in_place(piece)
        got[(0,) * len(combined)] = gate_rows.beside(piece, size, [piece] if number else [])
        bits = [upper[level] for level in combined]
        rows = []
        for slot in itertools.product((0, 1), repeat=len(combined)):
            rows.append(pick({xor(slot, flips): v for flips, v in got.items()}, bits))
        piece = jnp.concatenate(rows, axis=0)

    local = gate_up(piece, gate_weight, up_weight, gate_rows, 2 * gate_chunk)

    down_chunk = divisor(width, 256, 16)
    down_rows = Fetched(down_weight, down_chunk, width - down_chunk)
    for number, combined in enumerate(turns):
        last = number == len(turns) - 1
        got = {}
        for flips, mask in masks_of(combined)[1:]:
            got[flips] = swapped(local, mask)
        size = HADAMARD_BYTES[number] if number < len(HADAMARD_BYTES) else 0
        got[(0,) * len(combined)] = down_rows.beside(local, size, [local])
        turned = 0.0
        for flips, value in got.items():
            value = value.astype(jnp.float32)
            if not all(flips):
                value = jnp.where(odd[combined, flips], -value, value)
            turned += value
        if last:
            turned *= scale
        local = turned.astype(jnp.bfloat16)

    keep, send = down(local, down_weight, down_rows, down_chunk)
    terms = keep + swapped(send, 1).astype(jnp.float32)
    for combined in rounds[::-1][1:]:
        combined = combined[::-1]
        parts = terms.reshape((2,) * len(combined) + (-1, terms.shape[1]))
        bits = [upper[level] for level in combined]
        total = None
        for flips, mask in masks_of(combined):
            slots = {
                xor(slot, flips): parts[slot]
                for slot in itertools.product((0, 1), repeat=len(combined))
            }
            part = pick(slots, bits)
            if mask:
                part = swapped(part.astype(jnp.bfloat16), mask).astype(jnp.float32)
            total = part if total is None else total + part
        terms = total
    return terms.astype(jnp.bfloat16)


def solution(mesh):
    return jax.shard_map(
        per_device,
        mesh=mesh,
        in_specs=(
            P(("groups", "tensor"), None),
            P(None, "tensor"),
            P(None, "tensor"),
            P("tensor", None),
        ),
        out_specs=P(("groups", "tensor"), None),
        check_vma=False,
    )
```
